256 devices in a mesh: shard: 16 (over z_hi, y), example: 16 (over z_lo, x, core).
Axes of the slice: x: 4, y: 4, z: 8 (z_hi: 4, z_lo: 2; z = z_hi * 2 + z_lo), core: 2. Of those that a mesh axis runs over, the one named last changes fastest.
Arguments:
- train_in: bfloat16 [16, 512, 5120], P('example', 'shard'), may hold values from -6 to 6
- train_grad: bfloat16 [16, 512, 6912], P('example', 'shard'), may hold values from -6 to 6
- seq_lens: int32 [16], P('example'), may hold values from 128 to 512
- basis_in: bfloat16 [5120, 5120], P(None, 'shard'), may hold values from -0.078125 to 0.078125
- basis_out: bfloat16 [6912, 6912], P(None, 'example'), may hold values from -0.078125 to 0.078125
- eigvals: float32 [5120, 6912], P('shard', 'example'), may hold values from 0.01 to 90, as said below
- query_in: bfloat16 [32, 32, 5120], P('example'), may hold values from -6 to 6
- query_out: bfloat16 [32, 32, 6912], P('shard'), may hold values from -6 to 6
Outputs:
- scores: float32 [32, 16], P('shard', 'example')
The draws below stay inside these ranges and needn't reach their ends.
Inputs may be any that keep to these rules, and one draw needn't show every extreme that they name: `eigvals`: positive.
All inputs are finite; a program needn't handle non-finite values.
Results may differ from the reference program's by a relative error of at most 0.0051.
Values may be sent and summed in bfloat16 or wider, within the bound.
No kernel may reach another device: no remote copies, remote signals or barrier semaphores. Data moves between devices by JAX's collectives and lax.ppermute only.
A program may use at most 128 MiB of HBM per device.

```python
import math
import jax
import jax.numpy as jnp
from jax import lax

D = 5120
H = 6912
SEQLEN = 512
QUERIES = 32
RANK = 32
NSEQ = 16


def draw_eigvals(key, part):
    key = jax.random.fold_in(key, 11)
    row_ramp = jnp.arange(D, dtype=jnp.float32)[:, None] / D
    column_ramp = jnp.arange(H, dtype=jnp.float32)[None, :] / H
    levels = jax.random.uniform(key, (D, H), jnp.float32, math.log(0.01), math.log(10.0))
    return jnp.exp(levels) * jnp.exp(math.log(3.0) * (row_ramp + column_ramp))


def with_ends(entries, own_key, smallest, largest):
    longest = entries.shape.index(max(entries.shape))
    spots = []
    for shift in (0, 1):
        where = [jax.random.randint(jax.random.fold_in(own_key, axis), (), 0, length) for axis, length in enumerate(entries.shape)]
        where[longest] = (where[longest] + shift) % entries.shape[longest]
        spots.append(tuple(where))
    return entries.at[spots[0]].set(smallest).at[spots[1]].set(largest)


def block_levels(stream_key, dims, cuts, smallest, high):
    def one(dim, shards_of):
        steps = jax.random.uniform(jax.random.fold_in(jax.random.fold_in(stream_key, 6), dim), (shards_of,), jnp.float32, smallest / len(cuts), high / len(cuts))
        return jnp.repeat(jnp.exp(steps), dims[dim] // shards_of).reshape((-1,) + (1,) * (len(dims) - dim - 1))

    factor_of = one(*cuts[0])
    for cut in cuts[1:]:
        factor_of = factor_of * one(*cut)
    return factor_of


def noise(key, extent, scale, reach, split=(), kind=jnp.bfloat16):
    loudness = block_levels(key, extent, split, -0.22, 0.18) if split else 1.0
    drawn = jax.random.normal(key, extent, jnp.float32) * scale * loudness
    return jnp.minimum(jnp.maximum(drawn, -reach), reach).astype(kind)


def setup_inputs(seed: int = 0) -> dict:
    arg_keys = jax.random.split(jax.random.key(seed), 9)
    return {
        "train_in": noise(arg_keys[0], (NSEQ, SEQLEN, D), 1.0, 6.0, ((0, 16), (1, 16))),
        "train_grad": noise(arg_keys[1], (NSEQ, SEQLEN, H), 1.0, 6.0, ((0, 16), (1, 16))),
        "seq_lens": with_ends(jax.random.randint(arg_keys[2], (NSEQ,), SEQLEN // 4, SEQLEN + 1), jax.random.fold_in(arg_keys[2], 1), SEQLEN // 4, SEQLEN).astype(jnp.int32),
        "basis_in": noise(arg_keys[3], (D, D), D ** -0.5, 0.078125, ((1, 16),)),
        "basis_out": noise(arg_keys[4], (H, H), H ** -0.5, 0.078125, ((1, 16),)),
        "eigvals": draw_eigvals(jax.random.fold_in(arg_keys[8], 71), 0),
        "query_in": noise(arg_keys[6], (QUERIES, RANK, D), 1.0, 6.0, ((0, 16),)),
        "query_out": noise(arg_keys[7], (QUERIES, RANK, H), 1.0, 6.0, ((0, 16),)),
    }


def reference(train_in, train_grad, seq_lens, basis_in, basis_out, eigvals, query_in, query_out):
    positions = jnp.arange(SEQLEN, dtype=jnp.int32)
    keep_mask = positions[None, :] < seq_lens[:, None]
    masked_in = jnp.where(keep_mask[:, :, None], train_in, jnp.zeros_like(train_in))
    eigen_in = jnp.dot(masked_in.reshape(-1, D), basis_in, preferred_element_type=jnp.float32).astype(jnp.bfloat16).reshape(NSEQ, SEQLEN, D)
    eigen_out = jnp.dot(train_grad.reshape(-1, H), basis_out, preferred_element_type=jnp.float32).astype(jnp.bfloat16).reshape(NSEQ, SEQLEN, H)
    query_left = jnp.dot(query_in.reshape(-1, D), basis_in, preferred_element_type=jnp.float32).astype(jnp.bfloat16).reshape(QUERIES, RANK, D)
    query_right = jnp.dot(query_out.reshape(-1, H), basis_out, preferred_element_type=jnp.float32).astype(jnp.bfloat16).reshape(QUERIES, RANK, H)
    damping = 0.1 * jnp.mean(eigvals)
    out_wide = eigen_out.astype(jnp.float32)
    right_wide = query_right.astype(jnp.float32)
    block_size = math.gcd(D, 512)
    block_count = D // block_size

    def block_score(index):
        first_row = index * block_size
        left_block = lax.dynamic_slice_in_dim(eigen_in, first_row, block_size, 2).astype(jnp.float32)
        query_block = lax.dynamic_slice_in_dim(query_left, first_row, block_size, 2).astype(jnp.float32)
        eig_block = lax.dynamic_slice_in_dim(eigvals, first_row, block_size, 0)
        pair_grad = jnp.einsum('nti,ntj->nij', left_block, out_wide, precision=lax.Precision.HIGHEST)
        weighted = jnp.einsum('qri,qrj->qij', query_block, right_wide, precision=lax.Precision.HIGHEST) / (eig_block + damping)
        return jnp.einsum('nij,qij->qn', pair_grad, weighted, precision=lax.Precision.HIGHEST)
    summed = lax.optimization_barrier(jnp.sum(lax.map(block_score, jnp.arange(block_count, dtype=jnp.int32)), axis=0))
    normalizer = 1.0 / math.sqrt(RANK * D * H * SEQLEN)
    return summed * normalizer
```

```python
import math

import jax
import jax.numpy as jnp
from jax import lax
from jax.experimental import pallas as pl
from jax.experimental.pallas import tpu as pltpu
from jax.sharding import PartitionSpec as P

D = 5120
H = 6912
SEQLEN = 512
RANK = 32
NSEQ = 16
QUERIES = 32
BF16 = jnp.bfloat16
F32 = jnp.float32

Y_UP = [(i, i // 4 * 4 + (i + 1) % 4) for i in range(16)]
Y_DOWN = [(i, i // 4 * 4 + (i - 1) % 4) for i in range(16)]
Z_UP = [(i, (i + 4) % 16) for i in range(16)]
Z_DOWN = [(i, (i - 4) % 16) for i in range(16)]
AWAY = (0, -1, 1, 2)
COLS_Y_FIRST = 1792
SEQS_Y_FIRST = 6


def ring4(block, up, down):
    half = block.shape[0] // 2
    below = lax.ppermute(block, "shard", up)
    above = lax.ppermute(block, "shard", down)
    far_top = lax.ppermute(below[:half], "shard", up)
    far_bottom = lax.ppermute(above[half:], "shard", down)
    return [block, below, above, jnp.concatenate([far_top, far_bottom], 0)]


def gather_two_ways(y_first, z_first):
    step_z = ring4(z_first, Z_UP, Z_DOWN)
    step_y = ring4(y_first, Y_UP, Y_DOWN)
    out_z = ring4(jnp.concatenate(step_z, 0), Y_UP, Y_DOWN)
    out_y = ring4(jnp.concatenate(step_y, 0), Z_UP, Z_DOWN)
    ra, rb = y_first.shape[0], z_first.shape[0]
    blocks_y = [out_y[z][y * ra : (y + 1) * ra] for y in range(4) for z in range(4)]
    blocks_z = [out_z[y][z * rb : (z + 1) * rb] for y in range(4) for z in range(4)]
    return blocks_y, blocks_z


def three_terms(value):
    first = lax.reduce_precision(value, 8, 7)
    rest = value - first
    second = lax.reduce_precision(rest, 8, 7)
    return first, second, rest - second


def corner(value, shape):
    row = lax.broadcasted_iota(jnp.int32, shape, 0)
    col = lax.broadcasted_iota(jnp.int32, shape, 1)
    out = jnp.zeros(shape, F32)
    for k, term in enumerate(three_terms(value)):
        out = jnp.where((row == k) & (col == 0), term, out)
    return out.astype(BF16)


def score_kernel(place, ein, ql, eg, eout, qr, eig, out, inverse, right):
    n = pl.program_id(0)

    @pl.when(n == 0)
    def _():
        damping = (0.1 / (D * H)) * jnp.sum(eg[...].astype(F32))
        inverse[...] = 1.0 / (eig[...] + damping)
        for k in range(16):
            start = pl.multiple_of(place[k] * 64, 64)
            right[pl.ds(start, 64), :] = qr[k]
        out[...] = jnp.zeros_like(out)

    grads = eout[...].reshape(SEQLEN, eout.shape[-1])
    pair = lax.dot_general(ein[0], grads, (((0,), (0,)), ((), ())), preferred_element_type=F32)
    scaled = (pair * inverse[...]).astype(BF16)
    width = scaled.shape[1]
    sums = []
    for k in range(4):
        left = ql[4 * k : 4 * k + 4].reshape(256, ql.shape[-1])
        part = jnp.dot(left, scaled, preferred_element_type=F32)
        part = part * right[256 * k : 256 * k + 256, :].astype(F32)
        sums.append(jnp.sum(part.reshape(8, RANK, width), axis=1))
    total = jnp.sum(jnp.concatenate(sums, 0), axis=1, keepdims=True)
    lane = lax.broadcasted_iota(jnp.int32, out.shape, 1)
    out[...] = jnp.where(lane == n, total, out[...])


def score_call(place, ein, eout, qr, eigvals):
    di, dj = eigvals.shape
    return pl.pallas_call(
        score_kernel,
        grid=(NSEQ,),
        in_specs=[
            pl.BlockSpec(memory_space=pltpu.SMEM),
            pl.BlockSpec((1, SEQLEN, di), lambda n: (n, 0, 0)),
            pl.BlockSpec((16, 64, di), lambda n: (0, 8, 0)),
            pl.BlockSpec((16, 16, di), lambda n: (0, 36, 0)),
            pl.BlockSpec((16, 1, 32, dj), lambda n: (0, n, 0, 0)),
            pl.BlockSpec((16, 64, dj), lambda n: (0, 0, 0)),
            pl.BlockSpec((di, dj), lambda n: (0, 0)),
        ],
        out_specs=pl.BlockSpec((QUERIES, 128), lambda n: (0, 0)),
        out_shape=jax.ShapeDtypeStruct((QUERIES, 128), F32),
        scratch_shapes=[pltpu.VMEM((di, dj), F32), pltpu.VMEM((16 * 64, dj), BF16)],
        compiler_params=pltpu.CompilerParams(vmem_limit_bytes=40 * 1024 * 1024),
        cost_estimate=pl.CostEstimate(flops=8_000_000_000, bytes_accessed=16_000_000, transcendentals=0),
    )(place, ein, ein, ein, eout, qr, eigvals)


def shards(train_in, train_grad, seq_lens, basis_in, basis_out, eigvals, query_in, query_out):
    me = lax.axis_index("shard")
    place = jnp.stack(
        [(me // 4 + dz) % 4 * 4 + (me % 4 + dy) % 4 for dy in AWAY for dz in AWAY]
    ).astype(jnp.int32)

    grads_all = lax.all_gather(train_grad[0], "example", axis=0)

    rows = train_in[0]
    blocks_y, blocks_z = gather_two_ways(
        jnp.concatenate([rows[:, :COLS_Y_FIRST], corner(jnp.sum(eigvals), (32, 128))], 1),
        rows[:, COLS_Y_FIRST:],
    )
    eig_shard = sum(jnp.sum(b[:, COLS_Y_FIRST:].astype(F32)) for b in blocks_y)
    rows_y = jnp.concatenate([b[:, :COLS_Y_FIRST] for b in blocks_y], 0)
    rows_z = jnp.concatenate(blocks_z, 0)
    own_in = jnp.dot(rows_y, basis_in[:COLS_Y_FIRST], preferred_element_type=F32) + jnp.dot(
        rows_z, basis_in[COLS_Y_FIRST:], preferred_element_type=F32
    )
    token = (place[:, None] * 32 + jnp.arange(32, dtype=jnp.int32)[None, :]).reshape(SEQLEN, 1)
    own_in = jnp.where(token < seq_lens[0], own_in, 0.0).astype(BF16)
    query_left = jnp.dot(
        query_in.reshape(64, D), basis_in, preferred_element_type=F32
    ).astype(BF16)
    ein = lax.all_gather(
        jnp.concatenate([own_in, query_left, corner(eig_shard, (16, own_in.shape[1]))], 0),
        "example",
        axis=0,
    )

    query_right = jnp.dot(
        query_out.reshape(64, H), basis_out, preferred_element_type=F32
    ).astype(BF16)
    part_out = jnp.dot(
        grads_all.reshape(NSEQ * 32, H), basis_out, preferred_element_type=F32
    ).astype(BF16)
    cut = SEQS_Y_FIRST * 32
    blocks_y, blocks_z = gather_two_ways(
        part_out[:cut], jnp.concatenate([part_out[cut:], query_right], 0)
    )
    rest = NSEQ * 32 - cut
    eout = jnp.stack(
        [jnp.concatenate([a, b[:rest]], 0) for a, b in zip(blocks_y, blocks_z)]
    ).reshape(16, NSEQ, 32, part_out.shape[1])
    qr = jnp.stack([b[rest:] for b in blocks_z])

    partial = score_call(place, ein, eout, qr, eigvals)[:, :NSEQ]
    pieces = partial.reshape(16, 2, 16).transpose(0, 2, 1).reshape(256, 2)
    pieces = lax.all_to_all(pieces, ("shard", "example"), 0, 0, tiled=True)
    normalizer = 1.0 / math.sqrt(RANK * D * H * SEQLEN)
    return (jnp.sum(pieces, axis=0) * normalizer).reshape(2, 1)


def solution(mesh):
    placed = (
        P("example", "shard", None),
        P("example", "shard", None),
        P("example"),
        P(None, "shard"),
        P(None, "example"),
        P("shard", "example"),
        P("example", None, None),
        P("shard", None, None),
    )
    return jax.shard_map(
        shards, mesh=mesh, in_specs=placed, out_specs=P("shard", "example"), check_vma=False
    )
```

```python
import math

import jax
import jax.numpy as jnp
from jax import lax
from jax.experimental import pallas as pl
from jax.experimental.pallas import tpu as pltpu
from jax.sharding import PartitionSpec as P

D = 5120
H = 6912
SEQLEN = 512
RANK = 32
NSEQ = 16
QUERIES = 32
BF16 = jnp.bfloat16
F32 = jnp.float32

SHARD_Y = {d: [(i, i // 4 * 4 + (i + d) % 4) for i in range(16)] for d in (1, -1, 2)}
SHARD_Z = {d: [(i, (i + 4 * d) % 16) for i in range(16)] for d in (1, -1)}
EXAMPLE_X = {d: [(i, i // 8 * 8 + (i + 2 * d) % 8) for i in range(16)] for d in (1, -1)}
EXAMPLE_CORE = [(i, i ^ 1) for i in range(16)]
EXAMPLE_Z = [(i, i ^ 8) for i in range(16)]
AWAY = (0, -1, 1, 2)


def ring4(block, axis, steps):
    half = block.shape[0] // 2
    below = lax.ppermute(block, axis, steps[1])
    above = lax.ppermute(block, axis, steps[-1])
    far_top = lax.ppermute(below[:half], axis, steps[1])
    far_bottom = lax.ppermute(above[half:], axis, steps[-1])
    return [block, below, above, jnp.concatenate([far_top, far_bottom], 0)]


def exchange_y(blocks):
    sent = {d: lax.ppermute(blocks(d), "shard", SHARD_Y[d]) for d in (1, -1, 2)}
    return [blocks(0), sent[1], sent[-1], sent[2]]


def three_terms(value):
    first = lax.reduce_precision(value, 8, 7)
    rest = value - first
    second = lax.reduce_precision(rest, 8, 7)
    return first, second, rest - second


def corner(value, shape):
    row = lax.broadcasted_iota(jnp.int32, shape, 0)
    col = lax.broadcasted_iota(jnp.int32, shape, 1)
    out = jnp.zeros(shape, F32)
    for k, term in enumerate(three_terms(value)):
        out = jnp.where((row == k) & (col == 0), term, out)
    return out.astype(BF16)


def score_kernel(
    z_place, place, slot, ein, ql, eout, qr, eig, total_eig, out, inverse, right, grads, scaled
):
    n = pl.program_id(0)
    di = ein.shape[2]

    @pl.when(n == 0)
    def _():
        damping = (0.1 / (D * H)) * jnp.sum(total_eig[...].astype(F32))
        inverse[...] = 1.0 / (eig[...] + damping)
        for k in range(16):
            start = pl.multiple_of(place[k] * 64, 64)
            right[pl.ds(start, 64), :] = qr[64 * k : 64 * k + 64, :]
        out[...] = jnp.zeros_like(out)

    first = pl.multiple_of(slot[n] * 32, 32)
    for k in range(4):
        start = pl.multiple_of(z_place[k] * 32, 32)
        grads[pl.ds(start, 32), :] = eout[k, pl.ds(first, 32), :]
    for k in range(4):
        pair = jnp.dot(ein[0, k], grads[...], preferred_element_type=F32)
        scaled[di * k : di * k + di, :] = (pair * inverse[di * k : di * k + di, :]).astype(BF16)
    width = scaled.shape[1]
    sums = []
    for k in range(4):
        left = ql[4 * k : 4 * k + 4].reshape(256, ql.shape[-1])
        part = jnp.dot(left, scaled[...], preferred_element_type=F32)
        part = part * right[256 * k : 256 * k + 256, :].astype(F32)
        sums.append(jnp.sum(part.reshape(8, RANK, width), axis=1))
    total = jnp.sum(jnp.concatenate(sums, 0), axis=1, keepdims=True)
    lane = lax.broadcasted_iota(jnp.int32, out.shape, 1)
    out[...] = jnp.where(lane == n, total, out[...])


def score_call(z_place, place, slot, ein, ql, eout, qr, eig, total_eig):
    di, dj = ein.shape[2], eout.shape[2]

    def whole(x):
        return pl.BlockSpec(x.shape, lambda n, rank=x.ndim: (0,) * rank)

    return pl.pallas_call(
        score_kernel,
        grid=(NSEQ,),
        in_specs=[pl.BlockSpec(memory_space=pltpu.SMEM)] * 3
        + [pl.BlockSpec((1, 4, di, 128), lambda n: (n, 0, 0, 0))]
        + [whole(x) for x in (ql, eout, qr, eig, total_eig)],
        out_specs=pl.BlockSpec((QUERIES, 128), lambda n: (0, 0)),
        out_shape=jax.ShapeDtypeStruct((QUERIES, 128), F32),
        scratch_shapes=[
            pltpu.VMEM((4 * di, dj), F32),
            pltpu.VMEM((16 * 64, dj), BF16),
            pltpu.VMEM((128, dj), BF16),
            pltpu.VMEM((4 * di, dj), BF16),
        ],
        compiler_params=pltpu.CompilerParams(vmem_limit_bytes=48 * 1024 * 1024),
        cost_estimate=pl.CostEstimate(
            flops=20_000_000_000, bytes_accessed=16_000_000, transcendentals=0
        ),
    )(z_place, place, slot, ein, ql, eout, qr, eig, total_eig)


def shards(train_in, train_grad, seq_lens, basis_in, basis_out, eigvals, query_in, query_out):
    me = lax.axis_index("shard")
    example = lax.axis_index("example")
    my_z, my_y = me // 4, me % 4
    z_place = jnp.stack([(my_z + d) % 4 for d in AWAY]).astype(jnp.int32)
    place = jnp.stack(
        [(my_z + dz) % 4 * 4 + (my_y + dy) % 4 for dy in AWAY for dz in AWAY]
    ).astype(jnp.int32)
    seq = jnp.arange(NSEQ, dtype=jnp.int32)
    x_off = (seq // 2 - example // 2) % 4
    x_slot = jnp.where(x_off == 0, 0, jnp.where(x_off == 3, 1, jnp.where(x_off == 1, 2, 3)))
    slot = (
        ((seq % 2) != (example % 2)).astype(jnp.int32) * 8
        + x_slot * 2
        + ((seq // 8) != (example // 8)).astype(jnp.int32)
    ).astype(jnp.int32)

    rows_all = lax.all_gather(train_in[0], "shard", axis=0)

    block = jnp.concatenate([train_grad[0], corner(jnp.sum(eigvals), (32, 128))], 1)
    block = jnp.concatenate([block, lax.ppermute(block, "example", EXAMPLE_Z)], 0)
    block = jnp.concatenate(ring4(block, "example", EXAMPLE_X), 0)
    other = lax.ppermute(block, "example", EXAMPLE_CORE)
    eig_example = jnp.sum(block[:, H:].astype(F32)) + jnp.sum(other[:, H:].astype(F32))
    query_right = jnp.dot(
        query_out.reshape(64, H), basis_out, preferred_element_type=F32
    ).astype(BF16)
    part_out = [
        jnp.dot(b[:, :H], basis_out, preferred_element_type=F32).astype(BF16)
        for b in (block, other)
    ]
    dj = basis_out.shape[1]
    z_blocks = ring4(
        jnp.concatenate(part_out + [query_right, corner(eig_example, (32, dj))], 0),
        "shard",
        SHARD_Z,
    )
    eout = jnp.stack([b[: NSEQ * 32] for b in z_blocks])
    eig_z = sum(jnp.sum(b[NSEQ * 32 + 64 :].astype(F32)) for b in z_blocks)
    right_z = jnp.concatenate(
        [b[NSEQ * 32 : NSEQ * 32 + 64] for b in z_blocks] + [corner(eig_z, (16, dj))], 0
    )
    right_blocks = exchange_y(lambda d: right_z)
    qr = jnp.concatenate([b[:256] for b in right_blocks], 0)
    total_eig = jnp.concatenate([b[256:] for b in right_blocks], 0)

    eig = jnp.concatenate(ring4(eigvals, "shard", SHARD_Y), 0)
    query_left = jnp.dot(
        query_in.reshape(64, D), basis_in, preferred_element_type=F32
    ).astype(BF16)
    query_left = jnp.concatenate(exchange_y(lambda d: query_left), 1)
    query_left, rows_all = lax.optimization_barrier((query_left, rows_all))
    ql = lax.all_gather(query_left, "example", axis=0)

    own_in = jnp.dot(rows_all.reshape(SEQLEN, D), basis_in, preferred_element_type=F32)
    token = jnp.arange(SEQLEN, dtype=jnp.int32)[:, None]
    own_in = jnp.where(token < seq_lens[0], own_in, 0.0).astype(BF16)
    own_in = own_in.reshape(4, 4, 32, own_in.shape[1])

    def tokens_of(d):
        part = lax.dynamic_index_in_dim(own_in, (my_y + d) % 4, 1, keepdims=False)
        return part.reshape(128, own_in.shape[3])

    ein = jnp.stack([part.T for part in exchange_y(tokens_of)])
    ein, ql = lax.optimization_barrier((ein, ql))
    ein = lax.all_gather(ein, "example", axis=0)

    partial = score_call(z_place, place, slot, ein, ql, eout, qr, eig, total_eig)[:, :NSEQ]
    pieces = partial.reshape(16, 2, 16).transpose(0, 2, 1).reshape(256, 2)
    pieces = lax.all_to_all(pieces, ("shard", "example"), 0, 0, tiled=True)
    normalizer = 1.0 / math.sqrt(RANK * D * H * SEQLEN)
    return (jnp.sum(pieces, axis=0) * normalizer).reshape(2, 1)


def solution(mesh):
    placed = (
        P("example", "shard", None),
        P("example", "shard", None),
        P("example"),
        P(None, "shard"),
        P(None, "example"),
        P("shard", "example"),
        P("example", None, None),
        P("shard", None, None),
    )
    return jax.shard_map(
        shards, mesh=mesh, in_specs=placed, out_specs=P("shard", "example"), check_vma=False
    )
```

```python
import math

import jax
import jax.numpy as jnp
from jax import lax
from jax.experimental import pallas as pl
from jax.experimental.layout import Layout, with_layout_constraint
from jax.experimental.pallas import tpu as pltpu
from jax.sharding import PartitionSpec as P

D = 5120
H = 6912
SEQLEN = 512
RANK = 32
NSEQ = 16
QUERIES = 32
BF16 = jnp.bfloat16
F32 = jnp.float32

SHARD_Y = {d: [(i, i // 4 * 4 + (i + d) % 4) for i in range(16)] for d in (1, -1, 2)}
SHARD_Z = {d: [(i, (i + 4 * d) % 16) for i in range(16)] for d in (1, -1, 2)}
EXAMPLE_X = {d: [(i, i // 8 * 8 + (i + 2 * d) % 8) for i in range(16)] for d in (1, -1)}
EXAMPLE_CORE = [(i, i ^ 1) for i in range(16)]
EXAMPLE_Z = [(i, i ^ 8) for i in range(16)]
AWAY = (0, -1, 1, 2)


def ring4(block, axis, steps, cut):
    below = lax.ppermute(block, axis, steps[1])
    above = lax.ppermute(block, axis, steps[-1])
    far_top = lax.ppermute(below[:cut], axis, steps[1])
    far_bottom = lax.ppermute(above[cut:], axis, steps[-1])
    return [block, below, above, far_top, far_bottom]


def exchange(blocks, steps):
    sent = {d: lax.ppermute(blocks(d), "shard", steps[d]) for d in (1, -1, 2)}
    return [blocks(0), sent[1], sent[-1], sent[2]]


def three_terms(value):
    first = lax.reduce_precision(value, 8, 7)
    rest = value - first
    second = lax.reduce_precision(rest, 8, 7)
    return first, second, rest - second


def corner(value, shape):
    row = lax.broadcasted_iota(jnp.int32, shape, 0)
    col = lax.broadcasted_iota(jnp.int32, shape, 1)
    out = jnp.zeros(shape, F32)
    for k, term in enumerate(three_terms(value)):
        out = jnp.where((row == k) & (col == 0), term, out)
    return out.astype(BF16)


def score_kernel(
    z_place, place, slot, ein, ql,
    out_0, out_1, out_2, out_top, out_bottom,
    qr_0, qr_1, qr_2, qr_3,
    eig_0, eig_1, eig_2, eig_top, eig_bottom,
    out, inverse, right, grads, scaled,
):
    n = pl.program_id(0)
    di = ein.shape[2]

    @pl.when(n == 0)
    def _():
        damping = (0.1 / (D * H)) * jnp.sum(ql[:, 64:, :].astype(F32))
        row = 0
        for eig in (eig_0, eig_1, eig_2, eig_top, eig_bottom):
            inverse[row : row + eig.shape[0], :] = 1.0 / (eig[...] + damping)
            row += eig.shape[0]
        for ky, qr in enumerate((qr_0, qr_1, qr_2, qr_3)):
            for kz in range(4):
                start = pl.multiple_of(place[4 * ky + kz] * 64, 64)
                right[pl.ds(start, 64), :] = qr[64 * kz : 64 * kz + 64, :]
        out[...] = jnp.zeros_like(out)

    first = pl.multiple_of(slot[n] * 32, 32)
    starts = [pl.multiple_of(z_place[k] * 32, 32) for k in range(4)]
    for k, rows in enumerate((out_0, out_1, out_2)):
        grads[pl.ds(starts[k], 32), :] = rows[pl.ds(first, 32), :]
    cut = out_top.shape[0]

    @pl.when(first < cut)
    def _():
        grads[pl.ds(starts[3], 32), :] = out_top[pl.ds(first, 32), :]

    @pl.when(first >= cut)
    def _():
        grads[pl.ds(starts[3], 32), :] = out_bottom[pl.ds(first - cut, 32), :]

    for k in range(4):
        pair = jnp.dot(ein[0, k], grads[...], preferred_element_type=F32)
        scaled[di * k : di * k + di, :] = (pair * inverse[di * k : di * k + di, :]).astype(BF16)
    width = scaled.shape[1]
    sums = []
    for k in range(4):
        left = ql[4 * k : 4 * k + 4, :64, :].reshape(256, ql.shape[-1])
        part = jnp.dot(left, scaled[...], preferred_element_type=F32)
        part = part * right[256 * k : 256 * k + 256, :].astype(F32)
        sums.append(jnp.sum(part.reshape(8, RANK, width), axis=1))
    total = jnp.sum(jnp.concatenate(sums, 0), axis=1, keepdims=True)
    lane = lax.broadcasted_iota(jnp.int32, out.shape, 1)
    out[...] = jnp.where(lane == n, total, out[...])


def score_call(places, ein, rest):
    di, dj = ein.shape[2], rest[1].shape[1]

    def whole(x):
        return pl.BlockSpec(x.shape, lambda n, rank=x.ndim: (0,) * rank)

    return pl.pallas_call(
        score_kernel,
        grid=(NSEQ,),
        in_specs=[pl.BlockSpec(memory_space=pltpu.SMEM)] * 3
        + [pl.BlockSpec((1, 4, di, 128), lambda n: (n, 0, 0, 0))]
        + [whole(x) for x in rest],
        out_specs=pl.BlockSpec((QUERIES, 128), lambda n: (0, 0)),
        out_shape=jax.ShapeDtypeStruct((QUERIES, 128), F32),
        scratch_shapes=[
            pltpu.VMEM((4 * di, dj), F32),
            pltpu.VMEM((16 * 64, dj), BF16),
            pltpu.VMEM((128, dj), BF16),
            pltpu.VMEM((4 * di, dj), BF16),
        ],
        compiler_params=pltpu.CompilerParams(vmem_limit_bytes=48 * 1024 * 1024),
        cost_estimate=pl.CostEstimate(
            flops=20_000_000_000, bytes_accessed=16_000_000, transcendentals=0
        ),
    )(*places, ein, *rest)


def shards(train_in, train_grad, seq_lens, basis_in, basis_out, eigvals, query_in, query_out):
    me = lax.axis_index("shard")
    example = lax.axis_index("example")
    my_z, my_y = me // 4, me % 4
    z_place = jnp.stack([(my_z + d) % 4 for d in AWAY]).astype(jnp.int32)
    place = jnp.stack(
        [(my_z + dz) % 4 * 4 + (my_y + dy) % 4 for dy in AWAY for dz in AWAY]
    ).astype(jnp.int32)
    seq = jnp.arange(NSEQ, dtype=jnp.int32)
    x_off = (seq // 2 - example // 2) % 4
    x_slot = jnp.where(x_off == 0, 0, jnp.where(x_off == 3, 1, jnp.where(x_off == 1, 2, 3)))
    slot = (
        ((seq % 2) != (example % 2)).astype(jnp.int32) * 8
        + x_slot * 2
        + ((seq // 8) != (example // 8)).astype(jnp.int32)
    ).astype(jnp.int32)
    di, dj = eigvals.shape

    rows_all = lax.all_gather(train_in[0], "shard", axis=0)

    block = jnp.concatenate([train_grad[0], lax.ppermute(train_grad[0], "example", EXAMPLE_Z)], 0)
    block = jnp.concatenate(ring4(block, "example", EXAMPLE_X, 32), 0)
    other = lax.ppermute(block, "example", EXAMPLE_CORE)
    part_out = jnp.concatenate(
        [
            jnp.dot(b, basis_out, preferred_element_type=F32).astype(BF16)
            for b in (block, other)
        ],
        0,
    )
    part_out = with_layout_constraint(part_out, Layout(major_to_minor=(0, 1)))
    eout = ring4(part_out, "shard", SHARD_Z, 256)

    query_left = jnp.dot(
        query_in.reshape(64, D), basis_in, preferred_element_type=F32
    ).astype(BF16)
    query_left = jnp.concatenate([query_left, corner(jnp.sum(eigvals), (16, di))], 0)
    left_blocks = exchange(lambda d: query_left, SHARD_Y)
    eig_y = sum(jnp.sum(b[64:].astype(F32)) for b in left_blocks)
    query_right = jnp.dot(
        query_out.reshape(64, H), basis_out, preferred_element_type=F32
    ).astype(BF16)
    query_right = jnp.concatenate([query_right, corner(eig_y, (16, dj))], 0)
    right_blocks = exchange(lambda d: query_right, SHARD_Z)
    eig_shard = sum(jnp.sum(b[64:].astype(F32)) for b in right_blocks)
    right_z = jnp.concatenate([b[:64] for b in right_blocks], 0)
    right = exchange(lambda d: right_z, SHARD_Y)
    eig = ring4(eigvals, "shard", SHARD_Y, di // 2)
    left = jnp.concatenate(
        [jnp.concatenate([b[:64] for b in left_blocks], 1), corner(eig_shard, (16, 4 * di))], 0
    )
    left, rows_all = lax.optimization_barrier((left, rows_all))
    flag = jnp.isnan(part_out[-1, 0])
    left = jnp.where(flag, jnp.zeros_like(left), left)
    ql = lax.all_gather(left, "example", axis=0)

    own_in = jnp.dot(rows_all.reshape(SEQLEN, D), basis_in, preferred_element_type=F32)
    token = jnp.arange(SEQLEN, dtype=jnp.int32)[:, None]
    live = jnp.where(flag, 0, seq_lens[0])
    own_in = jnp.where(token < live, own_in, 0.0).astype(BF16)
    own_in = own_in.reshape(4, 4, 32, di)

    def tokens_of(d):
        part = lax.dynamic_index_in_dim(own_in, (my_y + d) % 4, 1, keepdims=False)
        return part.reshape(128, di)

    ein = jnp.stack([part.T for part in exchange(tokens_of, SHARD_Y)])
    ein, ql = lax.optimization_barrier((ein, ql))
    ein = lax.all_gather(ein, "example", axis=0)

    partial = score_call((z_place, place, slot), ein, [ql, *eout, *right, *eig])[:, :NSEQ]
    pieces = partial.reshape(16, 2, 16).transpose(0, 2, 1).reshape(256, 2)
    pieces = lax.all_to_all(pieces, ("shard", "example"), 0, 0, tiled=True)
    normalizer = 1.0 / math.sqrt(RANK * D * H * SEQLEN)
    return (jnp.sum(pieces, axis=0) * normalizer).reshape(2, 1)


def solution(mesh):
    placed = (
        P("example", "shard", None),
        P("example", "shard", None),
        P("example"),
        P(None, "shard"),
        P(None, "example"),
        P("shard", "example"),
        P("example", None, None),
        P("shard", None, None),
    )
    return jax.shard_map(
        shards, mesh=mesh, in_specs=placed, out_specs=P("shard", "example"), check_vma=False
    )
```

```python
import math

import jax
import jax.numpy as jnp
from jax import lax
from jax.experimental import pallas as pl
from jax.experimental.layout import Layout, with_layout_constraint
from jax.experimental.pallas import tpu as pltpu
from jax.sharding import PartitionSpec as P

D = 5120
H = 6912
SEQLEN = 512
RANK = 32
NSEQ = 16
QUERIES = 32
BF16 = jnp.bfloat16
F32 = jnp.float32

SHARD_Y = {d: [(i, i // 4 * 4 + (i + d) % 4) for i in range(16)] for d in (1, -1, 2)}
SHARD_Z = {d: [(i, (i + 4 * d) % 16) for i in range(16)] for d in (1, -1, 2)}
EXAMPLE_X = {d: [(i, i // 8 * 8 + (i + 2 * d) % 8) for i in range(16)] for d in (1, -1)}
EXAMPLE_CORE = [(i, i ^ 1) for i in range(16)]
EXAMPLE_Z = [(i, i ^ 8) for i in range(16)]
AWAY = (0, -1, 1, 2)


def ring4(block, axis, steps, cut):
    below = lax.ppermute(block, axis, steps[1])
    above = lax.ppermute(block, axis, steps[-1])
    far_top = lax.ppermute(below[:cut], axis, steps[1])
    far_bottom = lax.ppermute(above[cut:], axis, steps[-1])
    return [block, below, above, far_top, far_bottom]


def exchange(blocks, steps):
    sent = {d: lax.ppermute(blocks(d), "shard", steps[d]) for d in (1, -1, 2)}
    return [blocks(0), sent[1], sent[-1], sent[2]]


def three_terms(value):
    first = lax.reduce_precision(value, 8, 7)
    rest = value - first
    second = lax.reduce_precision(rest, 8, 7)
    return first, second, rest - second


def corner(value, shape):
    row = lax.broadcasted_iota(jnp.int32, shape, 0)
    col = lax.broadcasted_iota(jnp.int32, shape, 1)
    out = jnp.zeros(shape, F32)
    for k, term in enumerate(three_terms(value)):
        out = jnp.where((row == k) & (col == 0), term, out)
    return out.astype(BF16)


def score_kernel(
    z_place, place, slot, ein,
    ql_0, ql_1, ql_2, ql_top, ql_bottom,
    out_0, out_1, out_2, out_top, out_bottom,
    qr_0, qr_1, qr_2, qr_3,
    eig_0, eig_1, eig_2, eig_top, eig_bottom,
    out, inverse, left, ql_3, right, out_3, grads, scaled,
):
    n = pl.program_id(0)
    di = ein.shape[2]

    @pl.when(n == 0)
    def _():
        damping = (0.1 / (D * H)) * sum(
            jnp.sum(qr[256:, :].astype(F32)) for qr in (qr_0, qr_1, qr_2, qr_3)
        )
        row = 0
        for eig in (eig_0, eig_1, eig_2, eig_top, eig_bottom):
            inverse[row : row + eig.shape[0], :] = 1.0 / (eig[...] + damping)
            row += eig.shape[0]
        for ky, qr in enumerate((qr_0, qr_1, qr_2, qr_3)):
            for kz in range(4):
                start = pl.multiple_of(place[4 * ky + kz] * 64, 64)
                right[pl.ds(start, 64), :] = qr[64 * kz : 64 * kz + 64, :]
        for far, top, bottom in ((out_3, out_top, out_bottom), (ql_3, ql_top, ql_bottom)):
            far[: top.shape[0], :] = top[...]
            far[top.shape[0] :, :] = bottom[...]
        for e in range(NSEQ):
            first = pl.multiple_of(slot[e] * 32, 32)
            parts = [ql[pl.ds(first, 32), :] for ql in (ql_0, ql_1, ql_2, ql_3)]
            left[64 * e : 64 * e + 32, :] = jnp.concatenate([p[:, :di] for p in parts], 1)
            left[64 * e + 32 : 64 * e + 64, :] = jnp.concatenate([p[:, di:] for p in parts], 1)
        out[...] = jnp.zeros_like(out)

    first = pl.multiple_of(slot[n] * 32, 32)
    for k, rows in enumerate((out_0, out_1, out_2, out_3)):
        start = pl.multiple_of(z_place[k] * 32, 32)
        grads[pl.ds(start, 32), :] = rows[pl.ds(first, 32), :]
    for k in range(4):
        pair = jnp.dot(ein[0, k], grads[...], preferred_element_type=F32)
        scaled[di * k : di * k + di, :] = (pair * inverse[di * k : di * k + di, :]).astype(BF16)
    width = scaled.shape[1]
    sums = []
    for k in range(4):
        part = jnp.dot(
            left[256 * k : 256 * k + 256, :], scaled[...], preferred_element_type=F32
        )
        part = part * right[256 * k : 256 * k + 256, :].astype(F32)
        sums.append(jnp.sum(part.reshape(8, RANK, width), axis=1))
    total = jnp.sum(jnp.concatenate(sums, 0), axis=1, keepdims=True)
    lane = lax.broadcasted_iota(jnp.int32, out.shape, 1)
    out[...] = jnp.where(lane == n, total, out[...])


def score_call(places, ein, rest):
    di, dj = ein.shape[2], rest[5].shape[1]

    def whole(x):
        return pl.BlockSpec(x.shape, lambda n, rank=x.ndim: (0,) * rank)

    return pl.pallas_call(
        score_kernel,
        grid=(NSEQ,),
        in_specs=[pl.BlockSpec(memory_space=pltpu.SMEM)] * 3
        + [pl.BlockSpec((1, 4, di, 128), lambda n: (n, 0, 0, 0))]
        + [whole(x) for x in rest],
        out_specs=pl.BlockSpec((QUERIES, 128), lambda n: (0, 0)),
        out_shape=jax.ShapeDtypeStruct((QUERIES, 128), F32),
        scratch_shapes=[
            pltpu.VMEM((4 * di, dj), F32),
            pltpu.VMEM((16 * 64, 4 * di), BF16),
            pltpu.VMEM((NSEQ * 32, 2 * di), BF16),
            pltpu.VMEM((16 * 64, dj), BF16),
            pltpu.VMEM((NSEQ * 32, dj), BF16),
            pltpu.VMEM((128, dj), BF16),
            pltpu.VMEM((4 * di, dj), BF16),
        ],
        compiler_params=pltpu.CompilerParams(vmem_limit_bytes=48 * 1024 * 1024),
        cost_estimate=pl.CostEstimate(
            flops=20_000_000_000, bytes_accessed=16_000_000, transcendentals=0
        ),
    )(*places, ein, *rest)


def shards(train_in, train_grad, seq_lens, basis_in, basis_out, eigvals, query_in, query_out):
    me = lax.axis_index("shard")
    example = lax.axis_index("example")
    my_z, my_y = me // 4, me % 4
    z_place = jnp.stack([(my_z + d) % 4 for d in AWAY]).astype(jnp.int32)
    place = jnp.stack(
        [(my_z + dz) % 4 * 4 + (my_y + dy) % 4 for dy in AWAY for dz in AWAY]
    ).astype(jnp.int32)
    seq = jnp.arange(NSEQ, dtype=jnp.int32)
    x_off = (seq // 2 - example // 2) % 4
    x_slot = jnp.where(x_off == 0, 0, jnp.where(x_off == 3, 1, jnp.where(x_off == 1, 2, 3)))
    slot = (
        ((seq % 2) != (example % 2)).astype(jnp.int32) * 8
        + x_slot * 2
        + ((seq // 8) != (example // 8)).astype(jnp.int32)
    ).astype(jnp.int32)
    di, dj = eigvals.shape

    rows_all = lax.all_gather(train_in[0], "shard", axis=0)

    query_left = jnp.dot(
        query_in.reshape(64, D), basis_in, preferred_element_type=F32
    ).astype(BF16)
    block = jnp.concatenate(
        [train_grad[0], query_left[:32], query_left[32:], corner(jnp.sum(eigvals), (32, 128))], 1
    )
    block = jnp.concatenate([block, lax.ppermute(block, "example", EXAMPLE_Z)], 0)
    block = jnp.concatenate(ring4(block, "example", EXAMPLE_X, 32), 0)
    other = lax.ppermute(block, "example", EXAMPLE_CORE)
    part_out = jnp.concatenate(
        [
            jnp.dot(b[:, :H], basis_out, preferred_element_type=F32).astype(BF16)
            for b in (block, other)
        ],
        0,
    )
    part_out = with_layout_constraint(part_out, Layout(major_to_minor=(0, 1)))
    eout = ring4(part_out, "shard", SHARD_Z, 256)
    left = jnp.concatenate([b[:, H : H + 2 * di] for b in (block, other)], 0)
    left = ring4(left, "shard", SHARD_Y, 256)
    eig_example = jnp.sum(
        jnp.concatenate([b[:, H + 2 * di :] for b in (block, other)], 0).astype(F32)
    )

    query_right = jnp.dot(
        query_out.reshape(64, H), basis_out, preferred_element_type=F32
    ).astype(BF16)
    query_right = jnp.concatenate([query_right, corner(eig_example, (16, dj))], 0)
    right_blocks = exchange(lambda d: query_right, SHARD_Z)
    eig_z = jnp.sum(jnp.concatenate([b[64:] for b in right_blocks], 0).astype(F32))
    right_z = jnp.concatenate([b[:64] for b in right_blocks] + [corner(eig_z, (16, dj))], 0)
    right = exchange(lambda d: right_z, SHARD_Y)
    eig = ring4(eigvals, "shard", SHARD_Y, di // 2)
    flag = jnp.isnan(part_out[-1, 0])

    own_in = jnp.dot(rows_all.reshape(SEQLEN, D), basis_in, preferred_element_type=F32)
    token = jnp.arange(SEQLEN, dtype=jnp.int32)[:, None]
    live = jnp.where(flag, 0, seq_lens[0])
    own_in = jnp.where(token < live, own_in, 0.0).astype(BF16)
    own_in = own_in.reshape(4, 4, 32, di)

    def tokens_of(d):
        part = lax.dynamic_index_in_dim(own_in, (my_y + d) % 4, 1, keepdims=False)
        return part.reshape(128, di)

    ein = jnp.stack([part.T for part in exchange(tokens_of, SHARD_Y)])
    ein = jnp.where(jnp.isnan(eout[1][0, 0] + eout[2][0, 0]), jnp.zeros_like(ein), ein)
    ein = lax.all_gather(ein, "example", axis=0)

    partial = score_call((z_place, place, slot), ein, [*left, *eout, *right, *eig])[:, :NSEQ]
    pieces = partial.reshape(16, 2, 16).transpose(0, 2, 1).reshape(256, 2)
    pieces = lax.all_to_all(pieces, ("shard", "example"), 0, 0, tiled=True)
    normalizer = 1.0 / math.sqrt(RANK * D * H * SEQLEN)
    return (jnp.sum(pieces, axis=0) * normalizer).reshape(2, 1)


def solution(mesh):
    placed = (
        P("example", "shard", None),
        P("example", "shard", None),
        P("example"),
        P(None, "shard"),
        P(None, "example"),
        P("shard", "example"),
        P("example", None, None),
        P("shard", None, None),
    )
    return jax.shard_map(
        shards, mesh=mesh, in_specs=placed, out_specs=P("shard", "example"), check_vma=False
    )
```

```python
import math

import jax
import jax.numpy as jnp
from jax import lax
from jax.experimental import pallas as pl
from jax.experimental.layout import Layout, with_layout_constraint
from jax.experimental.pallas import tpu as pltpu
from jax.sharding import PartitionSpec as P

D = 5120
H = 6912
SEQLEN = 512
RANK = 32
NSEQ = 16
QUERIES = 32
BF16 = jnp.bfloat16
F32 = jnp.float32

SHARD_Y = {d: [(i, i // 4 * 4 + (i + d) % 4) for i in range(16)] for d in (1, -1)}
SHARD_Z = {d: [(i, (i + 4 * d) % 16) for i in range(16)] for d in (1, -1)}
EXAMPLE_X = {d: [(i, i // 8 * 8 + (i + 2 * d) % 8) for i in range(16)] for d in (1, -1)}
EXAMPLE_CORE = [(i, i ^ 1) for i in range(16)]
EXAMPLE_Z = [(i, i ^ 8) for i in range(16)]
AWAY = (0, -1, 1, 2)


def ring4(block, axis, steps, cut):
    below = lax.ppermute(block, axis, steps[1])
    above = lax.ppermute(block, axis, steps[-1])
    far_top = lax.ppermute(below[:cut], axis, steps[1])
    far_bottom = lax.ppermute(above[cut:], axis, steps[-1])
    return [block, below, above, far_top, far_bottom]


def three_terms(value):
    first = lax.reduce_precision(value, 8, 7)
    rest = value - first
    second = lax.reduce_precision(rest, 8, 7)
    return first, second, rest - second


def corner(value, shape):
    row = lax.broadcasted_iota(jnp.int32, shape, 0)
    col = lax.broadcasted_iota(jnp.int32, shape, 1)
    out = jnp.zeros(shape, F32)
    for k, term in enumerate(three_terms(value)):
        out = jnp.where((row == k) & (col == 0), term, out)
    return out.astype(BF16)


def score_kernel(
    place, slot, ein, ql,
    own_0, own_1, own_2, own_top, own_bottom,
    z_0, z_1, z_2, z_top, z_bottom,
    eig, out, inverse, left, right, own_3, z_3, grads,
):
    n = pl.program_id(0)
    dj = eig.shape[1]
    owns = (own_0, own_1, own_2, own_3)
    others = (z_0, z_1, z_2, z_3)
    size = own_0.shape[0]
    blocks = [(owns[y], 0) if z == 0 else (others[y], size * (z - 1)) for y in range(4) for z in range(4)]
    after = NSEQ * 32

    @pl.when(n == 0)
    def _():
        for far, top, bottom in ((own_3, own_top, own_bottom), (z_3, z_top, z_bottom)):
            far[: top.shape[0], :] = top[...]
            far[top.shape[0] :, :] = bottom[...]
        total = 0.0
        for k, (ref, row) in enumerate(blocks):
            start = pl.multiple_of(place[k] * 64, 64)
            right[pl.ds(start, 64), :] = ref[row + after : row + after + 64, :dj]
            total += jnp.sum(ref[row : row + 16, dj:].astype(F32))
        inverse[...] = 1.0 / (eig[...] + (0.1 / (D * H)) * total)
        for e in range(NSEQ):
            left[64 * e : 64 * e + 64, :] = ql[e].T[:64, :]
        out[...] = jnp.zeros_like(out)

    first = pl.multiple_of(slot[n] * 32, 32)
    for k, (ref, row) in enumerate(blocks):
        start = pl.multiple_of(place[k] * 32, 32)
        grads[pl.ds(start, 32), :] = ref[pl.ds(row + first, 32), :]
    pair = jnp.dot(ein[0], grads[...], preferred_element_type=F32)[:, :dj]
    scaled = (pair * inverse[...]).astype(BF16)
    width = scaled.shape[1]
    sums = []
    for k in range(4):
        part = jnp.dot(left[256 * k : 256 * k + 256, :], scaled, preferred_element_type=F32)
        part = part * right[256 * k : 256 * k + 256, :].astype(F32)
        sums.append(jnp.sum(part.reshape(8, RANK, width), axis=1))
    total = jnp.sum(jnp.concatenate(sums, 0), axis=1, keepdims=True)
    lane = lax.broadcasted_iota(jnp.int32, out.shape, 1)
    out[...] = jnp.where(lane == n, total, out[...])


def score_call(place, slot, ein, blocks, eigvals):
    di, dj = eigvals.shape

    def whole(x):
        return pl.BlockSpec(x.shape, lambda n, rank=x.ndim: (0,) * rank)

    return pl.pallas_call(
        score_kernel,
        grid=(NSEQ,),
        in_specs=[pl.BlockSpec(memory_space=pltpu.SMEM)] * 2
        + [
            pl.BlockSpec((1, di, SEQLEN), lambda n: (n, 0, 0)),
            pl.BlockSpec((16, di, 128), lambda n: (0, 0, 4)),
        ]
        + [whole(x) for x in (*blocks, eigvals)],
        out_specs=pl.BlockSpec((QUERIES, 128), lambda n: (0, 0)),
        out_shape=jax.ShapeDtypeStruct((QUERIES, 128), F32),
        scratch_shapes=[
            pltpu.VMEM((di, dj), F32),
            pltpu.VMEM((16 * 64, di), BF16),
            pltpu.VMEM((16 * 64, dj), BF16),
            pltpu.VMEM(blocks[0].shape, BF16),
            pltpu.VMEM(blocks[5].shape, BF16),
            pltpu.VMEM((SEQLEN, blocks[0].shape[1]), BF16),
        ],
        compiler_params=pltpu.CompilerParams(vmem_limit_bytes=48 * 1024 * 1024),
        cost_estimate=pl.CostEstimate(
            flops=10_000_000_000, bytes_accessed=16_000_000, transcendentals=0
        ),
    )(place, slot, ein, ein, *blocks, eigvals)


def shards(train_in, train_grad, seq_lens, basis_in, basis_out, eigvals, query_in, query_out):
    me = lax.axis_index("shard")
    example = lax.axis_index("example")
    place = jnp.stack(
        [(me // 4 + dz) % 4 * 4 + (me % 4 + dy) % 4 for dy in AWAY for dz in AWAY]
    ).astype(jnp.int32)
    seq = jnp.arange(NSEQ, dtype=jnp.int32)
    x_off = (seq // 2 - example // 2) % 4
    x_slot = jnp.where(x_off == 0, 0, jnp.where(x_off == 3, 1, jnp.where(x_off == 1, 2, 3)))
    slot = (
        ((seq % 2) != (example % 2)).astype(jnp.int32) * 8
        + x_slot * 2
        + ((seq // 8) != (example // 8)).astype(jnp.int32)
    ).astype(jnp.int32)
    di, dj = eigvals.shape
    row_major = Layout(major_to_minor=(0, 1))

    rows_all = lax.all_gather(train_in[0], "shard", axis=0)

    block = jnp.concatenate([train_grad[0], corner(jnp.sum(eigvals), (32, 128))], 1)
    block = jnp.concatenate([block, lax.ppermute(block, "example", EXAMPLE_Z)], 0)
    block = jnp.concatenate(ring4(block, "example", EXAMPLE_X, 32), 0)
    other = lax.ppermute(block, "example", EXAMPLE_CORE)
    eig_example = jnp.sum(
        jnp.concatenate([block[:, H:], other[:, H:]], 0).astype(F32)
    )
    query_right = jnp.dot(
        query_out.reshape(64, H), basis_out, preferred_element_type=F32
    ).astype(BF16)
    part_out = [
        jnp.dot(b[:, :H], basis_out, preferred_element_type=F32).astype(BF16)
        for b in (block, other)
    ]
    part_out = jnp.concatenate(part_out + [query_right], 0)
    sums = corner(eig_example, (part_out.shape[0], 512 - dj))
    part_out = with_layout_constraint(jnp.concatenate([part_out, sums], 1), row_major)
    z_blocks = ring4(part_out, "shard", SHARD_Z, 288)
    z_others = jnp.concatenate(z_blocks[1:], 0)
    blocks = ring4(part_out, "shard", SHARD_Y, 288) + ring4(z_others, "shard", SHARD_Y, 864)

    flag = jnp.isnan(part_out[256, 0])
    own_in = jnp.dot(rows_all.reshape(SEQLEN, D), basis_in, preferred_element_type=F32)
    token = jnp.arange(SEQLEN, dtype=jnp.int32)[:, None]
    live = jnp.where(flag, 0, seq_lens[0])
    own_in = jnp.where(token < live, own_in, 0.0).astype(BF16)
    query_left = jnp.dot(
        query_in.reshape(64, D), basis_in, preferred_element_type=F32
    ).astype(BF16)
    spare = jnp.zeros((di, 64), BF16)
    ein = jnp.concatenate([own_in.T, query_left.T, spare], 1)
    late = jnp.isnan(sum(b[0, 0] for b in z_blocks[1:] + blocks[1:3]))
    ein = jnp.where(late, jnp.zeros_like(ein), ein)
    ein = lax.all_gather(ein, "example", axis=0)

    partial = score_call(place, slot, ein, blocks, eigvals)[:, :NSEQ]
    pieces = partial.reshape(16, 2, 16).transpose(0, 2, 1).reshape(256, 2)
    pieces = lax.all_to_all(pieces, ("shard", "example"), 0, 0, tiled=True)
    normalizer = 1.0 / math.sqrt(RANK * D * H * SEQLEN)
    return (jnp.sum(pieces, axis=0) * normalizer).reshape(2, 1)


def solution(mesh):
    placed = (
        P("example", "shard", None),
        P("example", "shard", None),
        P("example"),
        P(None, "shard"),
        P(None, "example"),
        P("shard", "example"),
        P("example", None, None),
        P("shard", None, None),
    )
    return jax.shard_map(
        shards, mesh=mesh, in_specs=placed, out_specs=P("shard", "example"), check_vma=False
    )
```

```python
import math

import jax
import jax.numpy as jnp
from jax import lax
from jax.experimental import pallas as pl
from jax.experimental.layout import Layout, with_layout_constraint
from jax.experimental.pallas import tpu as pltpu
from jax.sharding import PartitionSpec as P

D = 5120
H = 6912
SEQLEN = 512
RANK = 32
NSEQ = 16
QUERIES = 32
BF16 = jnp.bfloat16
F32 = jnp.float32

SHARD_Y = {d: [(i, i // 4 * 4 + (i + d) % 4) for i in range(16)] for d in (1, -1)}
SHARD_Z = {d: [(i, (i + 4 * d) % 16) for i in range(16)] for d in (1, -1)}
EXAMPLE_X = {d: [(i, i // 8 * 8 + (i + 2 * d) % 8) for i in range(16)] for d in (1, -1)}
EXAMPLE_CORE = [(i, i ^ 1) for i in range(16)]
EXAMPLE_Z = [(i, i ^ 8) for i in range(16)]
AWAY = (0, -1, 1, 2)


def ring4(block, axis, steps, cut):
    below = lax.ppermute(block, axis, steps[1])
    above = lax.ppermute(block, axis, steps[-1])
    far_top = lax.ppermute(below[:cut], axis, steps[1])
    far_bottom = lax.ppermute(above[cut:], axis, steps[-1])
    return [block, below, above, far_top, far_bottom]


def three_terms(value):
    first = lax.reduce_precision(value, 8, 7)
    rest = value - first
    second = lax.reduce_precision(rest, 8, 7)
    return first, second, rest - second


def corner(value, shape):
    row = lax.broadcasted_iota(jnp.int32, shape, 0)
    col = lax.broadcasted_iota(jnp.int32, shape, 1)
    out = jnp.zeros(shape, F32)
    for k, term in enumerate(three_terms(value)):
        out = jnp.where((row == k) & (col == 0), term, out)
    return out.astype(BF16)


def score_kernel(
    place, slot, ein, ql,
    own_0, own_1, own_2, own_top, own_bottom,
    near_0, near_1, near_2, near_top, near_bottom,
    last_0, last_1, last_2, last_top, last_bottom,
    eig, out, inverse, left, right, own_3, near_3, last_3, grads,
):
    n = pl.program_id(0)
    dj = eig.shape[1]
    size = own_0.shape[0]
    blocks = []
    for own, near, last in (
        (own_0, near_0, last_0),
        (own_1, near_1, last_1),
        (own_2, near_2, last_2),
        (own_3, near_3, last_3),
    ):
        blocks += [(own, 0), (near, 0), (near, size), (last, 0)]
    after = NSEQ * 32

    @pl.when(n == 0)
    def _():
        for far, top, bottom in (
            (own_3, own_top, own_bottom),
            (near_3, near_top, near_bottom),
            (last_3, last_top, last_bottom),
        ):
            far[: top.shape[0], :] = top[...]
            far[top.shape[0] :, :] = bottom[...]
        for k, (ref, row) in enumerate(blocks):
            start = pl.multiple_of(place[k] * 64, 64)
            right[pl.ds(start, 64), :] = ref[row + after : row + after + 64, :dj]
        total = jnp.sum(ql[:, :, 64:].astype(F32))
        inverse[...] = 1.0 / (eig[...] + (0.1 / (D * H)) * total)
        for e in range(NSEQ):
            left[64 * e : 64 * e + 64, :] = ql[e].T[:64, :]
        out[...] = jnp.zeros_like(out)

    first = pl.multiple_of(slot[n] * 32, 32)
    for k, (ref, row) in enumerate(blocks):
        start = pl.multiple_of(place[k] * 32, 32)
        grads[pl.ds(start, 32), :] = ref[pl.ds(row + first, 32), :]
    pair = jnp.dot(ein[0], grads[...], preferred_element_type=F32)[:, :dj]
    scaled = (pair * inverse[...]).astype(BF16)
    width = scaled.shape[1]
    sums = []
    for k in range(4):
        part = jnp.dot(left[256 * k : 256 * k + 256, :], scaled, preferred_element_type=F32)
        part = part * right[256 * k : 256 * k + 256, :].astype(F32)
        sums.append(jnp.sum(part.reshape(8, RANK, width), axis=1))
    total = jnp.sum(jnp.concatenate(sums, 0), axis=1, keepdims=True)
    lane = lax.broadcasted_iota(jnp.int32, out.shape, 1)
    out[...] = jnp.where(lane == n, total, out[...])


def score_call(place, slot, ein, blocks, eigvals):
    di, dj = eigvals.shape

    def whole(x):
        return pl.BlockSpec(x.shape, lambda n, rank=x.ndim: (0,) * rank)

    return pl.pallas_call(
        score_kernel,
        grid=(NSEQ,),
        in_specs=[pl.BlockSpec(memory_space=pltpu.SMEM)] * 2
        + [
            pl.BlockSpec((1, di, SEQLEN), lambda n: (n, 0, 0)),
            pl.BlockSpec((16, di, 128), lambda n: (0, 0, 4)),
        ]
        + [whole(x) for x in (*blocks, eigvals)],
        out_specs=pl.BlockSpec((QUERIES, 128), lambda n: (0, 0)),
        out_shape=jax.ShapeDtypeStruct((QUERIES, 128), F32),
        scratch_shapes=[
            pltpu.VMEM((di, dj), F32),
            pltpu.VMEM((16 * 64, di), BF16),
            pltpu.VMEM((16 * 64, dj), BF16),
            pltpu.VMEM(blocks[0].shape, BF16),
            pltpu.VMEM(blocks[5].shape, BF16),
            pltpu.VMEM(blocks[10].shape, BF16),
            pltpu.VMEM((SEQLEN, blocks[0].shape[1]), BF16),
        ],
        compiler_params=pltpu.CompilerParams(vmem_limit_bytes=48 * 1024 * 1024),
        cost_estimate=pl.CostEstimate(
            flops=10_000_000_000, bytes_accessed=16_000_000, transcendentals=0
        ),
    )(place, slot, ein, ein, *blocks, eigvals)


def shards(train_in, train_grad, seq_lens, basis_in, basis_out, eigvals, query_in, query_out):
    me = lax.axis_index("shard")
    example = lax.axis_index("example")
    place = jnp.stack(
        [(me // 4 + dz) % 4 * 4 + (me % 4 + dy) % 4 for dy in AWAY for dz in AWAY]
    ).astype(jnp.int32)
    seq = jnp.arange(NSEQ, dtype=jnp.int32)
    x_off = (seq // 2 - example // 2) % 4
    x_slot = jnp.where(x_off == 0, 0, jnp.where(x_off == 3, 1, jnp.where(x_off == 1, 2, 3)))
    slot = (
        ((seq % 2) != (example % 2)).astype(jnp.int32) * 8
        + x_slot * 2
        + ((seq // 8) != (example // 8)).astype(jnp.int32)
    ).astype(jnp.int32)
    di, dj = eigvals.shape
    row_major = Layout(major_to_minor=(0, 1))

    rows_all = lax.all_gather(
        jnp.concatenate([train_in[0], corner(jnp.sum(eigvals), (32, 128))], 1), "shard", axis=0
    )

    block = jnp.concatenate([train_grad[0], lax.ppermute(train_grad[0], "example", EXAMPLE_Z)], 0)
    block = jnp.concatenate(ring4(block, "example", EXAMPLE_X, 32), 0)
    other = lax.ppermute(block, "example", EXAMPLE_CORE)
    query_right = jnp.dot(
        query_out.reshape(64, H), basis_out, preferred_element_type=F32
    ).astype(BF16)
    part_out = [
        jnp.dot(b, basis_out, preferred_element_type=F32).astype(BF16)
        for b in (block, other)
    ]
    part_out = jnp.concatenate(part_out + [query_right], 0)
    part_out = with_layout_constraint(jnp.pad(part_out, ((0, 0), (0, 512 - dj))), row_major)
    z_blocks = ring4(part_out, "shard", SHARD_Z, 288)
    near = jnp.concatenate(z_blocks[1:3], 0)
    last = jnp.concatenate(z_blocks[3:], 0)
    blocks = (
        ring4(part_out, "shard", SHARD_Y, 288)
        + ring4(near, "shard", SHARD_Y, 576)
        + ring4(last, "shard", SHARD_Y, 288)
    )

    flag = jnp.isnan(sum(b[0, 0] for b in z_blocks[1:3] + blocks[1:3]))
    own_in = jnp.dot(rows_all[:, :, :D].reshape(SEQLEN, D), basis_in, preferred_element_type=F32)
    token = jnp.arange(SEQLEN, dtype=jnp.int32)[:, None]
    live = jnp.where(flag, 0, seq_lens[0])
    own_in = jnp.where(token < live, own_in, 0.0).astype(BF16)
    query_left = jnp.dot(
        query_in.reshape(64, D), basis_in, preferred_element_type=F32
    ).astype(BF16)
    eig_shard = corner(jnp.sum(rows_all[:, :, D:].astype(F32)), (di, 64))
    ein = jnp.concatenate([own_in.T, query_left.T, eig_shard], 1)
    ein = lax.all_gather(ein, "example", axis=0)

    partial = score_call(place, slot, ein, blocks, eigvals)[:, :NSEQ]
    pieces = partial.reshape(16, 2, 16).transpose(0, 2, 1).reshape(256, 2)
    pieces = lax.all_to_all(pieces, ("shard", "example"), 0, 0, tiled=True)
    normalizer = 1.0 / math.sqrt(RANK * D * H * SEQLEN)
    return (jnp.sum(pieces, axis=0) * normalizer).reshape(2, 1)


def solution(mesh):
    placed = (
        P("example", "shard", None),
        P("example", "shard", None),
        P("example"),
        P(None, "shard"),
        P(None, "example"),
        P("shard", "example"),
        P("example", None, None),
        P("shard", None, None),
    )
    return jax.shard_map(
        shards, mesh=mesh, in_specs=placed, out_specs=P("shard", "example"), check_vma=False
    )
```

```python
import math

import jax
import jax.numpy as jnp
from jax import lax
from jax.experimental import pallas as pl
from jax.experimental.layout import Layout, with_layout_constraint
from jax.experimental.pallas import tpu as pltpu
from jax.sharding import PartitionSpec as P

D = 5120
H = 6912
SEQLEN = 512
RANK = 32
NSEQ = 16
QUERIES = 32
BF16 = jnp.bfloat16
F32 = jnp.float32

SHARD_Y = {d: [(i, i // 4 * 4 + (i + d) % 4) for i in range(16)] for d in (1, -1)}
SHARD_Z = {d: [(i, (i + 4 * d) % 16) for i in range(16)] for d in (1, -1)}
EXAMPLE_X = {d: [(i, i // 8 * 8 + (i + 2 * d) % 8) for i in range(16)] for d in (1, -1)}
EXAMPLE_CORE = [(i, i ^ 1) for i in range(16)]
EXAMPLE_Z = [(i, i ^ 8) for i in range(16)]
AWAY = (0, -1, 1, 2)


def ring4(block, axis, steps, cut):
    below = lax.ppermute(block, axis, steps[1])
    above = lax.ppermute(block, axis, steps[-1])
    far_top = lax.ppermute(below[:cut], axis, steps[1])
    far_bottom = lax.ppermute(above[cut:], axis, steps[-1])
    return [block, below, above, far_top, far_bottom]


def three_terms(value):
    first = lax.reduce_precision(value, 8, 7)
    rest = value - first
    second = lax.reduce_precision(rest, 8, 7)
    return first, second, rest - second


def corner(value, shape):
    row = lax.broadcasted_iota(jnp.int32, shape, 0)
    col = lax.broadcasted_iota(jnp.int32, shape, 1)
    out = jnp.zeros(shape, F32)
    for k, term in enumerate(three_terms(value)):
        out = jnp.where((row == k) & (col == 0), term, out)
    return out.astype(BF16)


def score_kernel(
    place, slot, ein, ql,
    own_0, own_1, own_2, own_top, own_bottom,
    near_0, near_1, near_2, near_top, near_bottom,
    last_0, last_1, last_2, last_top, last_bottom,
    eig, out, inverse, left, right, own_3, near_3, last_3, grads,
):
    n = pl.program_id(0)
    dj = eig.shape[1]
    size = own_0.shape[0]
    blocks = []
    for own, near, last in (
        (own_0, near_0, last_0),
        (own_1, near_1, last_1),
        (own_2, near_2, last_2),
        (own_3, near_3, last_3),
    ):
        blocks += [(own, 0), (near, 0), (near, size), (last, 0)]
    after = NSEQ * 32

    @pl.when(n == 0)
    def _():
        for far, top, bottom in (
            (own_3, own_top, own_bottom),
            (near_3, near_top, near_bottom),
            (last_3, last_top, last_bottom),
        ):
            far[: top.shape[0], :] = top[...]
            far[top.shape[0] :, :] = bottom[...]
        for k, (ref, row) in enumerate(blocks):
            start = pl.multiple_of(place[k] * 64, 64)
            right[pl.ds(start, 64), :] = ref[row + after : row + after + 64, :dj]
        total = jnp.sum(ql[:, :, 64:].astype(F32))
        inverse[...] = 1.0 / (eig[...] + (0.1 / (D * H)) * total)
        for e in range(NSEQ):
            left[64 * e : 64 * e + 64, :] = ql[e].T[:64, :]
        out[...] = jnp.zeros_like(out)

    first = pl.multiple_of(slot[n] * 32, 32)
    for k, (ref, row) in enumerate(blocks):
        start = pl.multiple_of(place[k] * 16, 16)
        rows = ref[pl.ds(row + first, 32), :]
        grads[pl.ds(start, 16), :] = rows[:16]
        grads[256 + 16 * k : 256 + 16 * k + 16, :] = rows[16:]
    pair = jnp.dot(ein[0], grads[...], preferred_element_type=F32)[:, :dj]
    scaled = (pair * inverse[...]).astype(BF16)
    width = scaled.shape[1]
    sums = []
    for k in range(4):
        part = jnp.dot(left[256 * k : 256 * k + 256, :], scaled, preferred_element_type=F32)
        part = part * right[256 * k : 256 * k + 256, :].astype(F32)
        sums.append(jnp.sum(part.reshape(8, RANK, width), axis=1))
    total = jnp.sum(jnp.concatenate(sums, 0), axis=1, keepdims=True)
    lane = lax.broadcasted_iota(jnp.int32, out.shape, 1)
    out[...] = jnp.where(lane == n, total, out[...])


def score_call(place, slot, ein, blocks, eigvals):
    di, dj = eigvals.shape

    def whole(x):
        return pl.BlockSpec(x.shape, lambda n, rank=x.ndim: (0,) * rank)

    return pl.pallas_call(
        score_kernel,
        grid=(NSEQ,),
        in_specs=[pl.BlockSpec(memory_space=pltpu.SMEM)] * 2
        + [
            pl.BlockSpec((1, di, SEQLEN), lambda n: (n, 0, 0)),
            pl.BlockSpec((16, di, 128), lambda n: (0, 0, 4)),
        ]
        + [whole(x) for x in (*blocks, eigvals)],
        out_specs=pl.BlockSpec((QUERIES, 128), lambda n: (0, 0)),
        out_shape=jax.ShapeDtypeStruct((QUERIES, 128), F32),
        scratch_shapes=[
            pltpu.VMEM((di, dj), F32),
            pltpu.VMEM((16 * 64, di), BF16),
            pltpu.VMEM((16 * 64, dj), BF16),
            pltpu.VMEM(blocks[0].shape, BF16),
            pltpu.VMEM(blocks[5].shape, BF16),
            pltpu.VMEM(blocks[10].shape, BF16),
            pltpu.VMEM((SEQLEN, blocks[0].shape[1]), BF16),
        ],
        compiler_params=pltpu.CompilerParams(vmem_limit_bytes=48 * 1024 * 1024),
        cost_estimate=pl.CostEstimate(
            flops=10_000_000_000, bytes_accessed=16_000_000, transcendentals=0
        ),
    )(place, slot, ein, ein, *blocks, eigvals)


def shards(train_in, train_grad, seq_lens, basis_in, basis_out, eigvals, query_in, query_out):
    me = lax.axis_index("shard")
    example = lax.axis_index("example")
    place = jnp.stack(
        [(me // 4 + dz) % 4 * 4 + (me % 4 + dy) % 4 for dy in AWAY for dz in AWAY]
    ).astype(jnp.int32)
    seq = jnp.arange(NSEQ, dtype=jnp.int32)
    x_off = (seq // 2 - example // 2) % 4
    x_slot = jnp.where(x_off == 0, 0, jnp.where(x_off == 3, 1, jnp.where(x_off == 1, 2, 3)))
    slot = (
        ((seq % 2) != (example % 2)).astype(jnp.int32) * 8
        + x_slot * 2
        + ((seq // 8) != (example // 8)).astype(jnp.int32)
    ).astype(jnp.int32)
    di, dj = eigvals.shape
    row_major = Layout(major_to_minor=(0, 1))

    rows_all = lax.all_gather(
        jnp.concatenate([train_in[0, :16], corner(jnp.sum(eigvals), (16, 128))], 1),
        "shard",
        axis=0,
    )
    rows_ring = jnp.concatenate(ring4(train_in[0, 16:], "shard", SHARD_Z, 8), 0)
    rows_ring = jnp.concatenate(ring4(rows_ring, "shard", SHARD_Y, 32), 0)

    block = jnp.concatenate([train_grad[0], lax.ppermute(train_grad[0], "example", EXAMPLE_Z)], 0)
    block = jnp.concatenate(ring4(block, "example", EXAMPLE_X, 32), 0)
    other = lax.ppermute(block, "example", EXAMPLE_CORE)
    query_right = jnp.dot(
        query_out.reshape(64, H), basis_out, preferred_element_type=F32
    ).astype(BF16)
    part_out = [
        jnp.dot(b, basis_out, preferred_element_type=F32).astype(BF16)
        for b in (block, other)
    ]
    part_out = jnp.concatenate(part_out + [query_right], 0)
    part_out = with_layout_constraint(jnp.pad(part_out, ((0, 0), (0, 512 - dj))), row_major)
    z_blocks = ring4(part_out, "shard", SHARD_Z, 288)
    near = jnp.concatenate(z_blocks[1:3], 0)
    last = jnp.concatenate(z_blocks[3:], 0)
    blocks = (
        ring4(part_out, "shard", SHARD_Y, 288)
        + ring4(near, "shard", SHARD_Y, 576)
        + ring4(last, "shard", SHARD_Y, 288)
    )

    own_in = jnp.concatenate(
        [
            jnp.dot(rows, basis_in, preferred_element_type=F32)
            for rows in (rows_all[:, :, :D].reshape(256, D), rows_ring)
        ],
        0,
    )
    half = jnp.arange(16, dtype=jnp.int32)
    token = jnp.concatenate(
        [(half[:, None] * 32 + half).reshape(256), (place[:, None] * 32 + 16 + half).reshape(256)]
    )
    own_in = jnp.where(token[:, None] < seq_lens[0], own_in, 0.0).astype(BF16)
    query_left = jnp.dot(
        query_in.reshape(64, D), basis_in, preferred_element_type=F32
    ).astype(BF16)
    eig_shard = corner(jnp.sum(rows_all[:, :, D:].astype(F32)), (di, 64))
    ein = jnp.concatenate([own_in.T, query_left.T, eig_shard], 1)
    flag = jnp.isnan(sum(b[0, 0] for b in z_blocks[1:3] + blocks[1:3]))
    ein = jnp.where(flag, jnp.zeros_like(ein), ein)
    ein = lax.all_gather(ein, "example", axis=0)

    partial = score_call(place, slot, ein, blocks, eigvals)[:, :NSEQ]
    pieces = partial.reshape(16, 2, 16).transpose(0, 2, 1).reshape(256, 2)
    pieces = lax.all_to_all(pieces, ("shard", "example"), 0, 0, tiled=True)
    normalizer = 1.0 / math.sqrt(RANK * D * H * SEQLEN)
    return (jnp.sum(pieces, axis=0) * normalizer).reshape(2, 1)


def solution(mesh):
    placed = (
        P("example", "shard", None),
        P("example", "shard", None),
        P("example"),
        P(None, "shard"),
        P(None, "example"),
        P("shard", "example"),
        P("example", None, None),
        P("shard", None, None),
    )
    return jax.shard_map(
        shards, mesh=mesh, in_specs=placed, out_specs=P("shard", "example"), check_vma=False
    )
```

```python
import math

import jax
import jax.numpy as jnp
from jax import lax
from jax.experimental import pallas as pl
from jax.experimental.layout import Layout, with_layout_constraint
from jax.experimental.pallas import tpu as pltpu
from jax.sharding import PartitionSpec as P

D = 5120
H = 6912
SEQLEN = 512
RANK = 32
NSEQ = 16
QUERIES = 32
BF16 = jnp.bfloat16
F32 = jnp.float32

SHARD_Y = {d: [(i, i // 4 * 4 + (i + d) % 4) for i in range(16)] for d in (1, -1)}
SHARD_Z = {d: [(i, (i + 4 * d) % 16) for i in range(16)] for d in (1, -1)}
EXAMPLE_X = {d: [(i, i // 8 * 8 + (i + 2 * d) % 8) for i in range(16)] for d in (1, -1)}
EXAMPLE_CORE = [(i, i ^ 1) for i in range(16)]
EXAMPLE_Z = [(i, i ^ 8) for i in range(16)]
AWAY = (0, -1, 1, 2)


def ring4(block, axis, steps, cut):
    below = lax.ppermute(block, axis, steps[1])
    above = lax.ppermute(block, axis, steps[-1])
    far_top = lax.ppermute(below[:cut], axis, steps[1])
    far_bottom = lax.ppermute(above[cut:], axis, steps[-1])
    return [block, below, above, far_top, far_bottom]


def three_terms(value):
    first = lax.reduce_precision(value, 8, 7)
    rest = value - first
    second = lax.reduce_precision(rest, 8, 7)
    return first, second, rest - second


def corner(value, shape):
    row = lax.broadcasted_iota(jnp.int32, shape, 0)
    col = lax.broadcasted_iota(jnp.int32, shape, 1)
    out = jnp.zeros(shape, F32)
    for k, term in enumerate(three_terms(value)):
        out = jnp.where((row == k) & (col == 0), term, out)
    return out.astype(BF16)


def score_kernel(
    place, slot, ein, ql,
    own_0, own_1, own_2, own_top, own_bottom,
    near_0, near_1, near_2, near_top, near_bottom,
    last_0, last_1, last_2, last_top, last_bottom,
    eig, out, inverse, left, right, own_3, near_3, last_3, grads,
):
    n = pl.program_id(0)
    dj = eig.shape[1]
    size = own_0.shape[0]
    blocks = []
    for own, near, last in (
        (own_0, near_0, last_0),
        (own_1, near_1, last_1),
        (own_2, near_2, last_2),
        (own_3, near_3, last_3),
    ):
        blocks += [(own, 0), (near, 0), (near, size), (last, 0)]
    after = NSEQ * 32

    @pl.when(n == 0)
    def _():
        for far, top, bottom in (
            (own_3, own_top, own_bottom),
            (near_3, near_top, near_bottom),
            (last_3, last_top, last_bottom),
        ):
            far[: top.shape[0], :] = top[...]
            far[top.shape[0] :, :] = bottom[...]
        for k, (ref, row) in enumerate(blocks):
            start = pl.multiple_of(place[k] * 64, 64)
            right[pl.ds(start, 64), :] = ref[row + after : row + after + 64, :dj]
        total = jnp.sum(ql[:, :, 64:].astype(F32))
        inverse[...] = 1.0 / (eig[...] + (0.1 / (D * H)) * total)
        for e in range(NSEQ):
            left[64 * e : 64 * e + 64, :] = ql[e].T[:64, :]
        out[...] = jnp.zeros_like(out)

    first = pl.multiple_of(slot[n] * 32, 32)
    for k, (ref, row) in enumerate(blocks):
        start = pl.multiple_of(place[k] * 16, 16)
        rows = ref[pl.ds(row + first, 32), :]
        grads[pl.ds(start, 16), :] = rows[:16]
        grads[256 + 16 * k : 256 + 16 * k + 16, :] = rows[16:]
    pair = jnp.dot(ein[0], grads[...], preferred_element_type=F32)[:, :dj]
    scaled = (pair * inverse[...]).astype(BF16)
    width = scaled.shape[1]
    sums = []
    for k in range(4):
        part = jnp.dot(left[256 * k : 256 * k + 256, :], scaled, preferred_element_type=F32)
        part = part * right[256 * k : 256 * k + 256, :].astype(F32)
        sums.append(jnp.sum(part.reshape(8, RANK, width), axis=1))
    total = jnp.sum(jnp.concatenate(sums, 0), axis=1, keepdims=True)
    lane = lax.broadcasted_iota(jnp.int32, out.shape, 1)
    out[...] = jnp.where(lane == n, total, out[...])


def score_call(place, slot, ein, blocks, eigvals):
    di, dj = eigvals.shape

    return pl.pallas_call(
        score_kernel,
        grid=(NSEQ,),
        in_specs=[pl.BlockSpec(memory_space=pltpu.SMEM)] * 2
        + [
            pl.BlockSpec((1, di, SEQLEN), lambda n: (n, 0, 0)),
            pl.BlockSpec((16, di, 128), lambda n: (0, 0, 4)),
        ]
        + [pl.BlockSpec(memory_space=pltpu.VMEM)] * (len(blocks) + 1),
        out_specs=pl.BlockSpec((QUERIES, 128), lambda n: (0, 0)),
        out_shape=jax.ShapeDtypeStruct((QUERIES, 128), F32),
        scratch_shapes=[
            pltpu.VMEM((di, dj), F32),
            pltpu.VMEM((16 * 64, di), BF16),
            pltpu.VMEM((16 * 64, dj), BF16),
            pltpu.VMEM(blocks[0].shape, BF16),
            pltpu.VMEM(blocks[5].shape, BF16),
            pltpu.VMEM(blocks[10].shape, BF16),
            pltpu.VMEM((SEQLEN, blocks[0].shape[1]), BF16),
        ],
        compiler_params=pltpu.CompilerParams(vmem_limit_bytes=32 * 1024 * 1024),
        cost_estimate=pl.CostEstimate(
            flops=10_000_000_000, bytes_accessed=16_000_000, transcendentals=0
        ),
    )(place, slot, ein, ein, *blocks, eigvals)


def shards(train_in, train_grad, seq_lens, basis_in, basis_out, eigvals, query_in, query_out):
    me = lax.axis_index("shard")
    example = lax.axis_index("example")
    place = jnp.stack(
        [(me // 4 + dz) % 4 * 4 + (me % 4 + dy) % 4 for dy in AWAY for dz in AWAY]
    ).astype(jnp.int32)
    seq = jnp.arange(NSEQ, dtype=jnp.int32)
    x_off = (seq // 2 - example // 2) % 4
    x_slot = jnp.where(x_off == 0, 0, jnp.where(x_off == 3, 1, jnp.where(x_off == 1, 2, 3)))
    slot = (
        ((seq % 2) != (example % 2)).astype(jnp.int32) * 8
        + x_slot * 2
        + ((seq // 8) != (example // 8)).astype(jnp.int32)
    ).astype(jnp.int32)
    di, dj = eigvals.shape
    row_major = Layout(major_to_minor=(0, 1))

    rows_all = lax.all_gather(
        jnp.concatenate([train_in[0, :16], corner(jnp.sum(eigvals), (16, 128))], 1),
        "shard",
        axis=0,
    )
    zl_block = lax.ppermute(train_grad[0], "example", EXAMPLE_Z)
    block = jnp.concatenate([train_grad[0], zl_block], 0)
    block = jnp.concatenate(ring4(block, "example", EXAMPLE_X, 32), 0)
    other = lax.ppermute(block, "example", EXAMPLE_CORE)
    rows_ring = jnp.where(
        jnp.isnan(zl_block[0, 0]), jnp.zeros((16, D), BF16), train_in[0, 16:]
    )
    rows_ring = jnp.concatenate(ring4(rows_ring, "shard", SHARD_Z, 8), 0)
    rows_ring = jnp.where(jnp.isnan(other[0, 0]), jnp.zeros_like(rows_ring), rows_ring)
    rows_ring = jnp.concatenate(ring4(rows_ring, "shard", SHARD_Y, 32), 0)

    query_right = jnp.dot(
        query_out.reshape(64, H), basis_out, preferred_element_type=F32
    ).astype(BF16)
    part_out = [
        jnp.dot(b, basis_out, preferred_element_type=F32).astype(BF16)
        for b in (block, other)
    ]
    part_out = jnp.concatenate(part_out + [query_right], 0)
    part_out = with_layout_constraint(jnp.pad(part_out, ((0, 0), (0, 512 - dj))), row_major)
    z_blocks = ring4(part_out, "shard", SHARD_Z, 288)
    near = jnp.concatenate(z_blocks[1:3], 0)
    last = jnp.concatenate(z_blocks[3:], 0)
    blocks = (
        ring4(part_out, "shard", SHARD_Y, 288)
        + ring4(near, "shard", SHARD_Y, 576)
        + ring4(last, "shard", SHARD_Y, 288)
    )

    own_in = jnp.concatenate(
        [
            jnp.dot(rows, basis_in, preferred_element_type=F32)
            for rows in (rows_all[:, :, :D].reshape(256, D), rows_ring)
        ],
        0,
    )
    half = jnp.arange(16, dtype=jnp.int32)
    token = jnp.concatenate(
        [(half[:, None] * 32 + half).reshape(256), (place[:, None] * 32 + 16 + half).reshape(256)]
    )
    own_in = jnp.where(token[:, None] < seq_lens[0], own_in, 0.0).astype(BF16)
    query_left = jnp.dot(
        query_in.reshape(64, D), basis_in, preferred_element_type=F32
    ).astype(BF16)
    eig_shard = corner(jnp.sum(rows_all[:, :, D:].astype(F32)), (di, 64))
    ein = jnp.concatenate([own_in.T, query_left.T, eig_shard], 1)
    flag = jnp.isnan(sum(b[0, 0] for b in z_blocks[1:3] + blocks[3:5]))
    ein = jnp.where(flag, jnp.zeros_like(ein), ein)
    ein = lax.all_gather(ein, "example", axis=0)

    partial = score_call(place, slot, ein, blocks, eigvals)[:, :NSEQ]
    pieces = partial.reshape(16, 2, 16).transpose(0, 2, 1).reshape(256, 2)
    pieces = lax.all_to_all(pieces, ("shard", "example"), 0, 0, tiled=True)
    normalizer = 1.0 / math.sqrt(RANK * D * H * SEQLEN)
    return (jnp.sum(pieces, axis=0) * normalizer).reshape(2, 1)


def solution(mesh):
    placed = (
        P("example", "shard", None),
        P("example", "shard", None),
        P("example"),
        P(None, "shard"),
        P(None, "example"),
        P("shard", "example"),
        P("example", None, None),
        P("shard", None, None),
    )
    return jax.shard_map(
        shards, mesh=mesh, in_specs=placed, out_specs=P("shard", "example"), check_vma=False
    )
```

```python
import math

import jax
import jax.numpy as jnp
from jax import lax
from jax.experimental import pallas as pl
from jax.experimental.layout import Layout, with_layout_constraint
from jax.experimental.pallas import tpu as pltpu
from jax.sharding import PartitionSpec as P

D = 5120
H = 6912
SEQLEN = 512
RANK = 32
NSEQ = 16
QUERIES = 32
BF16 = jnp.bfloat16
F32 = jnp.float32

SHARD_Y = {d: [(i, i // 4 * 4 + (i + d) % 4) for i in range(16)] for d in (1, -1)}
SHARD_Z = {d: [(i, (i + 4 * d) % 16) for i in range(16)] for d in (1, -1)}
EXAMPLE_X = {d: [(i, i // 8 * 8 + (i + 2 * d) % 8) for i in range(16)] for d in (1, -1)}
EXAMPLE_CORE = [(i, i ^ 1) for i in range(16)]
EXAMPLE_Z = [(i, i ^ 8) for i in range(16)]
AWAY = (0, -1, 1, 2)


def after(block, *others):
    flag = jnp.isnan(sum(other[0, 0] for other in others))
    return jnp.where(flag, jnp.zeros_like(block), block)


def hop(block, axis, steps):
    return lax.ppermute(block, axis, steps[1]), lax.ppermute(block, axis, steps[-1])


def relay(near, axis, steps, cut, first=()):
    top, bottom = near[0][:cut], near[1][cut:]
    if first:
        top, bottom = after(top, *first), after(bottom, *first)
    return lax.ppermute(top, axis, steps[1]), lax.ppermute(bottom, axis, steps[-1])


def ring4(block, axis, steps, cut):
    near = hop(block, axis, steps)
    return [block, *near, *relay(near, axis, steps, cut)]


def three_terms(value):
    first = lax.reduce_precision(value, 8, 7)
    rest = value - first
    second = lax.reduce_precision(rest, 8, 7)
    return first, second, rest - second


def corner(value, shape):
    row = lax.broadcasted_iota(jnp.int32, shape, 0)
    col = lax.broadcasted_iota(jnp.int32, shape, 1)
    out = jnp.zeros(shape, F32)
    for k, term in enumerate(three_terms(value)):
        out = jnp.where((row == k) & (col == 0), term, out)
    return out.astype(BF16)


def score_kernel(
    place, slot, ein, ql,
    own_0, own_1, own_2, own_top, own_bottom,
    near_0, near_1, near_2, near_top, near_bottom,
    last_0, last_1, last_2, last_top, last_bottom,
    eig, out, inverse, left, right, own_3, near_3, last_3, grads,
):
    n = pl.program_id(0)
    dj = eig.shape[1]
    size = own_0.shape[0]
    blocks = []
    for own, near, last in (
        (own_0, near_0, last_0),
        (own_1, near_1, last_1),
        (own_2, near_2, last_2),
        (own_3, near_3, last_3),
    ):
        blocks += [(own, 0), (near, 0), (near, size), (last, 0)]
    gradient_rows = NSEQ * 32

    @pl.when(n == 0)
    def _():
        for far, top, bottom in (
            (own_3, own_top, own_bottom),
            (near_3, near_top, near_bottom),
            (last_3, last_top, last_bottom),
        ):
            far[: top.shape[0], :] = top[...]
            far[top.shape[0] :, :] = bottom[...]
        for k, (ref, row) in enumerate(blocks):
            start = pl.multiple_of(place[k] * 64, 64)
            right[pl.ds(start, 64), :] = ref[row + gradient_rows : row + size, :dj]
        total = jnp.sum(ql[:, :, 64:].astype(F32))
        inverse[...] = 1.0 / (eig[...] + (0.1 / (D * H)) * total)
        for e in range(NSEQ):
            left[64 * e : 64 * e + 64, :] = ql[e].T[:64, :]
        out[...] = jnp.zeros_like(out)

    first = pl.multiple_of(slot[n] * 32, 32)
    for k, (ref, row) in enumerate(blocks):
        start = pl.multiple_of(place[k] * 16, 16)
        rows = ref[pl.ds(row + first, 32), :]
        grads[pl.ds(start, 16), :] = rows[:16]
        grads[256 + 16 * k : 256 + 16 * k + 16, :] = rows[16:]
    pair = jnp.dot(ein[0], grads[...], preferred_element_type=F32)[:, :dj]
    scaled = (pair * inverse[...]).astype(BF16)
    width = scaled.shape[1]
    sums = []
    for k in range(4):
        part = jnp.dot(left[256 * k : 256 * k + 256, :], scaled, preferred_element_type=F32)
        part = part * right[256 * k : 256 * k + 256, :].astype(F32)
        sums.append(jnp.sum(part.reshape(8, RANK, width), axis=1))
    total = jnp.sum(jnp.concatenate(sums, 0), axis=1, keepdims=True)
    lane = lax.broadcasted_iota(jnp.int32, out.shape, 1)
    out[...] = jnp.where(lane == n, total, out[...])


def score_call(place, slot, ein, blocks, eigvals):
    di, dj = eigvals.shape

    def whole(x):
        return pl.BlockSpec(
            x.shape, lambda n, rank=x.ndim: (0,) * rank, pipeline_mode=pl.Buffered(1)
        )

    return pl.pallas_call(
        score_kernel,
        grid=(NSEQ,),
        in_specs=[pl.BlockSpec(memory_space=pltpu.SMEM)] * 2
        + [
            pl.BlockSpec((1, di, SEQLEN), lambda n: (n, 0, 0)),
            pl.BlockSpec((16, di, 128), lambda n: (0, 0, 4)),
        ]
        + [whole(x) for x in (*blocks, eigvals)],
        out_specs=pl.BlockSpec((QUERIES, 128), lambda n: (0, 0)),
        out_shape=jax.ShapeDtypeStruct((QUERIES, 128), F32),
        scratch_shapes=[
            pltpu.VMEM((di, dj), F32),
            pltpu.VMEM((16 * 64, di), BF16),
            pltpu.VMEM((16 * 64, dj), BF16),
            pltpu.VMEM(blocks[0].shape, BF16),
            pltpu.VMEM(blocks[5].shape, BF16),
            pltpu.VMEM(blocks[10].shape, BF16),
            pltpu.VMEM((SEQLEN, blocks[0].shape[1]), BF16),
        ],
        compiler_params=pltpu.CompilerParams(vmem_limit_bytes=28 * 1024 * 1024),
        cost_estimate=pl.CostEstimate(
            flops=10_000_000_000, bytes_accessed=16_000_000, transcendentals=0
        ),
    )(place, slot, ein, ein, *blocks, eigvals)


def shards(train_in, train_grad, seq_lens, basis_in, basis_out, eigvals, query_in, query_out):
    me = lax.axis_index("shard")
    example = lax.axis_index("example")
    place = jnp.stack(
        [(me // 4 + dz) % 4 * 4 + (me % 4 + dy) % 4 for dy in AWAY for dz in AWAY]
    ).astype(jnp.int32)
    seq = jnp.arange(NSEQ, dtype=jnp.int32)
    x_off = (seq // 2 - example // 2) % 4
    x_slot = jnp.where(x_off == 0, 0, jnp.where(x_off == 3, 1, jnp.where(x_off == 1, 2, 3)))
    slot = (
        ((seq % 2) != (example % 2)).astype(jnp.int32) * 8
        + x_slot * 2
        + ((seq // 8) != (example // 8)).astype(jnp.int32)
    ).astype(jnp.int32)
    di, dj = eigvals.shape
    row_major = Layout(major_to_minor=(0, 1))

    rows_all = lax.all_gather(
        jnp.concatenate([train_in[0, :16], corner(jnp.sum(eigvals), (16, 128))], 1),
        "shard",
        axis=0,
    )
    block = jnp.concatenate([train_grad[0], lax.ppermute(train_grad[0], "example", EXAMPLE_Z)], 0)
    rows_own = train_in[0, 16:]
    rows_near = hop(rows_own, "shard", SHARD_Z)
    near = hop(block, "example", EXAMPLE_X)
    rows_far = relay(rows_near, "shard", SHARD_Z, 8, near)
    far = relay(near, "example", EXAMPLE_X, 32, rows_near)
    block = jnp.concatenate([block, *near, after(far[0], *rows_far), far[1]], 0)
    rows_z = jnp.concatenate([rows_own, *rows_near, *rows_far], 0)
    rows_y = hop(rows_z, "shard", SHARD_Y)
    other = lax.ppermute(block, "example", EXAMPLE_CORE)
    query_right = jnp.dot(
        query_out.reshape(64, H), basis_out, preferred_element_type=F32
    ).astype(BF16)
    part_out = [
        jnp.dot(b, basis_out, preferred_element_type=F32).astype(BF16)
        for b in (block, other)
    ]
    rows_ring = jnp.concatenate(
        [rows_z, *rows_y, *relay(rows_y, "shard", SHARD_Y, 32, part_out[1:])], 0
    )
    part_out = jnp.concatenate(part_out + [after(query_right, *rows_y)], 0)
    part_out = with_layout_constraint(jnp.pad(part_out, ((0, 0), (0, 512 - dj))), row_major)
    z_blocks = ring4(part_out, "shard", SHARD_Z, 288)
    near = jnp.concatenate(z_blocks[1:3], 0)
    last = jnp.concatenate(z_blocks[3:], 0)
    blocks = (
        ring4(part_out, "shard", SHARD_Y, 288)
        + ring4(near, "shard", SHARD_Y, 576)
        + ring4(last, "shard", SHARD_Y, 288)
    )

    own_in = jnp.concatenate(
        [
            jnp.dot(rows, basis_in, preferred_element_type=F32)
            for rows in (rows_all[:, :, :D].reshape(256, D), rows_ring)
        ],
        0,
    )
    half = jnp.arange(16, dtype=jnp.int32)
    token = jnp.concatenate(
        [(half[:, None] * 32 + half).reshape(256), (place[:, None] * 32 + 16 + half).reshape(256)]
    )
    own_in = jnp.where(token[:, None] < seq_lens[0], own_in, 0.0).astype(BF16)
    query_left = jnp.dot(
        query_in.reshape(64, D), basis_in, preferred_element_type=F32
    ).astype(BF16)
    eig_shard = corner(jnp.sum(rows_all[:, :, D:].astype(F32)), (di, 64))
    ein = jnp.concatenate([own_in.T, query_left.T, eig_shard], 1)
    ein = after(ein, *z_blocks[1:3], *blocks[3:5])
    ein = lax.all_gather(ein, "example", axis=0)

    partial = score_call(place, slot, ein, blocks, eigvals)[:, :NSEQ]
    pieces = partial.reshape(16, 2, 16).transpose(0, 2, 1).reshape(256, 2)
    pieces = lax.all_to_all(pieces, ("shard", "example"), 0, 0, tiled=True)
    normalizer = 1.0 / math.sqrt(RANK * D * H * SEQLEN)
    return (jnp.sum(pieces, axis=0) * normalizer).reshape(2, 1)


def solution(mesh):
    placed = (
        P("example", "shard", None),
        P("example", "shard", None),
        P("example"),
        P(None, "shard"),
        P(None, "example"),
        P("shard", "example"),
        P("example", None, None),
        P("shard", None, None),
    )
    return jax.shard_map(
        shards, mesh=mesh, in_specs=placed, out_specs=P("shard", "example"), check_vma=False
    )
```

```python
import math

import jax
import jax.numpy as jnp
from jax import lax
from jax.experimental import pallas as pl
from jax.experimental.layout import Layout, with_layout_constraint
from jax.experimental.pallas import tpu as pltpu
from jax.sharding import PartitionSpec as P

D = 5120
H = 6912
SEQLEN = 512
RANK = 32
NSEQ = 16
QUERIES = 32
BF16 = jnp.bfloat16
F32 = jnp.float32

SHARD_Y = {d: [(i, i // 4 * 4 + (i + d) % 4) for i in range(16)] for d in (1, -1)}
SHARD_Z = {d: [(i, (i + 4 * d) % 16) for i in range(16)] for d in (1, -1)}
EXAMPLE_X = {d: [(i, i // 8 * 8 + (i + 2 * d) % 8) for i in range(16)] for d in (1, -1)}
EXAMPLE_CORE = [(i, i ^ 1) for i in range(16)]
EXAMPLE_Z = [(i, i ^ 8) for i in range(16)]
AWAY = (0, -1, 1, 2)


def ring4(block, axis, steps, cut):
    below = lax.ppermute(block, axis, steps[1])
    above = lax.ppermute(block, axis, steps[-1])
    far_top = lax.ppermute(below[:cut], axis, steps[1])
    far_bottom = lax.ppermute(above[cut:], axis, steps[-1])
    return [block, below, above, far_top, far_bottom]


def three_terms(value):
    first = lax.reduce_precision(value, 8, 7)
    rest = value - first
    second = lax.reduce_precision(rest, 8, 7)
    return first, second, rest - second


def corner(value, shape):
    row = lax.broadcasted_iota(jnp.int32, shape, 0)
    col = lax.broadcasted_iota(jnp.int32, shape, 1)
    out = jnp.zeros(shape, F32)
    for k, term in enumerate(three_terms(value)):
        out = jnp.where((row == k) & (col == 0), term, out)
    return out.astype(BF16)


def score_kernel(
    place, slot, ein, ql,
    own_0, own_1, own_2, own_top, own_bottom,
    near_0, near_1, near_2, near_top, near_bottom,
    last_0, last_1, last_2, last_top, last_bottom,
    eig, out, inverse, left, right, own_3, near_3, last_3, grads,
):
    n = pl.program_id(0)
    dj = eig.shape[1]
    size = own_0.shape[0]
    blocks = []
    for own, near, last in (
        (own_0, near_0, last_0),
        (own_1, near_1, last_1),
        (own_2, near_2, last_2),
        (own_3, near_3, last_3),
    ):
        blocks += [(own, 0), (near, 0), (near, size), (last, 0)]
    after = NSEQ * 32

    @pl.when(n == 0)
    def _():
        for far, top, bottom in (
            (own_3, own_top, own_bottom),
            (near_3, near_top, near_bottom),
            (last_3, last_top, last_bottom),
        ):
            far[: top.shape[0], :] = top[...]
            far[top.shape[0] :, :] = bottom[...]
        for k, (ref, row) in enumerate(blocks):
            start = pl.multiple_of(place[k] * 64, 64)
            right[pl.ds(start, 64), :] = ref[row + after : row + after + 64, :dj]
        total = jnp.sum(ql[:, :, 64:].astype(F32))
        inverse[...] = 1.0 / (eig[...] + (0.1 / (D * H)) * total)
        for e in range(NSEQ):
            left[64 * e : 64 * e + 64, :] = ql[e].T[:64, :]
        out[...] = jnp.zeros_like(out)

    first = pl.multiple_of(slot[n] * 32, 32)
    for k, (ref, row) in enumerate(blocks):
        start = pl.multiple_of(place[k] * 16, 16)
        rows = ref[pl.ds(row + first, 32), :]
        grads[pl.ds(start, 16), :] = rows[:16]
        grads[256 + 16 * k : 256 + 16 * k + 16, :] = rows[16:]
    pair = jnp.dot(ein[0], grads[...], preferred_element_type=F32)[:, :dj]
    scaled = (pair * inverse[...]).astype(BF16)
    width = scaled.shape[1]
    sums = []
    for k in range(4):
        part = jnp.dot(left[256 * k : 256 * k + 256, :], scaled, preferred_element_type=F32)
        part = part * right[256 * k : 256 * k + 256, :].astype(F32)
        sums.append(jnp.sum(part.reshape(8, RANK, width), axis=1))
    total = jnp.sum(jnp.concatenate(sums, 0), axis=1, keepdims=True)
    lane = lax.broadcasted_iota(jnp.int32, out.shape, 1)
    out[...] = jnp.where(lane == n, total, out[...])


def score_call(place, slot, ein, blocks, eigvals):
    di, dj = eigvals.shape

    def whole(x):
        return pl.BlockSpec(x.shape, lambda n, rank=x.ndim: (0,) * rank)

    return pl.pallas_call(
        score_kernel,
        grid=(NSEQ,),
        in_specs=[pl.BlockSpec(memory_space=pltpu.SMEM)] * 2
        + [
            pl.BlockSpec((1, di, SEQLEN), lambda n: (n, 0, 0)),
            pl.BlockSpec((16, di, 128), lambda n: (0, 0, 4)),
        ]
        + [whole(x) for x in (*blocks, eigvals)],
        out_specs=pl.BlockSpec((QUERIES, 128), lambda n: (0, 0)),
        out_shape=jax.ShapeDtypeStruct((QUERIES, 128), F32),
        scratch_shapes=[
            pltpu.VMEM((di, dj), F32),
            pltpu.VMEM((16 * 64, di), BF16),
            pltpu.VMEM((16 * 64, dj), BF16),
            pltpu.VMEM(blocks[0].shape, BF16),
            pltpu.VMEM(blocks[5].shape, BF16),
            pltpu.VMEM(blocks[10].shape, BF16),
            pltpu.VMEM((SEQLEN, blocks[0].shape[1]), BF16),
        ],
        compiler_params=pltpu.CompilerParams(vmem_limit_bytes=48 * 1024 * 1024),
        cost_estimate=pl.CostEstimate(
            flops=10_000_000_000, bytes_accessed=16_000_000, transcendentals=0
        ),
    )(place, slot, ein, ein, *blocks, eigvals)


def shards(train_in, train_grad, seq_lens, basis_in, basis_out, eigvals, query_in, query_out):
    me = lax.axis_index("shard")
    example = lax.axis_index("example")
    place = jnp.stack(
        [(me // 4 + dz) % 4 * 4 + (me % 4 + dy) % 4 for dy in AWAY for dz in AWAY]
    ).astype(jnp.int32)
    seq = jnp.arange(NSEQ, dtype=jnp.int32)
    x_off = (seq // 2 - example // 2) % 4
    x_slot = jnp.where(x_off == 0, 0, jnp.where(x_off == 3, 1, jnp.where(x_off == 1, 2, 3)))
    slot = (
        ((seq % 2) != (example % 2)).astype(jnp.int32) * 8
        + x_slot * 2
        + ((seq // 8) != (example // 8)).astype(jnp.int32)
    ).astype(jnp.int32)
    di, dj = eigvals.shape
    row_major = Layout(major_to_minor=(0, 1))

    rows_all = lax.all_gather(
        jnp.concatenate([train_in[0, :16], corner(jnp.sum(eigvals), (16, 128))], 1),
        "shard",
        axis=0,
    )
    rows_ring = jnp.concatenate(ring4(train_in[0, 16:], "shard", SHARD_Z, 8), 0)
    rows_y = ring4(rows_ring, "shard", SHARD_Y, 32)
    rows_ring = jnp.concatenate(rows_y, 0)

    block = jnp.concatenate([train_grad[0], lax.ppermute(train_grad[0], "example", EXAMPLE_Z)], 0)
    block = jnp.concatenate(ring4(block, "example", EXAMPLE_X, 32), 0)
    other = lax.ppermute(block, "example", EXAMPLE_CORE)
    query_right = jnp.dot(
        jnp.where(jnp.isnan(rows_y[1][0, 0]), jnp.zeros((64, H), BF16), query_out.reshape(64, H)),
        basis_out,
        preferred_element_type=F32,
    ).astype(BF16)
    part_out = [
        jnp.dot(b, basis_out, preferred_element_type=F32).astype(BF16)
        for b in (block, other)
    ]
    part_out = jnp.concatenate(part_out + [query_right], 0)
    part_out = with_layout_constraint(jnp.pad(part_out, ((0, 0), (0, 512 - dj))), row_major)
    z_blocks = ring4(part_out, "shard", SHARD_Z, 288)
    near = jnp.concatenate(z_blocks[1:3], 0)
    last = jnp.concatenate(z_blocks[3:], 0)
    blocks = (
        ring4(part_out, "shard", SHARD_Y, 288)
        + ring4(near, "shard", SHARD_Y, 576)
        + ring4(last, "shard", SHARD_Y, 288)
    )

    own_in = jnp.concatenate(
        [
            jnp.dot(rows, basis_in, preferred_element_type=F32)
            for rows in (rows_all[:, :, :D].reshape(256, D), rows_ring)
        ],
        0,
    )
    half = jnp.arange(16, dtype=jnp.int32)
    token = jnp.concatenate(
        [(half[:, None] * 32 + half).reshape(256), (place[:, None] * 32 + 16 + half).reshape(256)]
    )
    own_in = jnp.where(token[:, None] < seq_lens[0], own_in, 0.0).astype(BF16)
    query_left = jnp.dot(
        query_in.reshape(64, D), basis_in, preferred_element_type=F32
    ).astype(BF16)
    eig_shard = corner(jnp.sum(rows_all[:, :, D:].astype(F32)), (di, 64))
    ein = jnp.concatenate([own_in.T, query_left.T, eig_shard], 1)
    flag = jnp.isnan(sum(b[0, 0] for b in z_blocks[1:3] + blocks[1:3]))
    ein = jnp.where(flag, jnp.zeros_like(ein), ein)
    ein = lax.all_gather(ein, "example", axis=0)

    partial = score_call(place, slot, ein, blocks, eigvals)[:, :NSEQ]
    pieces = partial.reshape(16, 2, 16).transpose(0, 2, 1).reshape(256, 2)
    pieces = lax.all_to_all(pieces, ("shard", "example"), 0, 0, tiled=True)
    normalizer = 1.0 / math.sqrt(RANK * D * H * SEQLEN)
    return (jnp.sum(pieces, axis=0) * normalizer).reshape(2, 1)


def solution(mesh):
    placed = (
        P("example", "shard", None),
        P("example", "shard", None),
        P("example"),
        P(None, "shard"),
        P(None, "example"),
        P("shard", "example"),
        P("example", None, None),
        P("shard", None, None),
    )
    return jax.shard_map(
        shards, mesh=mesh, in_specs=placed, out_specs=P("shard", "example"), check_vma=False
    )
```

```python
import math

import jax
import jax.numpy as jnp
from jax import lax
from jax.experimental import pallas as pl
from jax.experimental.layout import Layout, with_layout_constraint
from jax.experimental.pallas import tpu as pltpu
from jax.sharding import PartitionSpec as P

D = 5120
H = 6912
SEQLEN = 512
RANK = 32
NSEQ = 16
QUERIES = 32
BF16 = jnp.bfloat16
F32 = jnp.float32

SHARD_Y = {d: [(i, i // 4 * 4 + (i + d) % 4) for i in range(16)] for d in (1, -1)}
SHARD_Z = {d: [(i, (i + 4 * d) % 16) for i in range(16)] for d in (1, -1)}
EXAMPLE_X = {d: [(i, i // 8 * 8 + (i + 2 * d) % 8) for i in range(16)] for d in (1, -1)}
EXAMPLE_CORE = [(i, i ^ 1) for i in range(16)]
EXAMPLE_Z = [(i, i ^ 8) for i in range(16)]
AWAY = (0, -1, 1, 2)


def ring4(block, axis, steps, cut):
    below = lax.ppermute(block, axis, steps[1])
    above = lax.ppermute(block, axis, steps[-1])
    far_top = lax.ppermute(below[:cut], axis, steps[1])
    far_bottom = lax.ppermute(above[cut:], axis, steps[-1])
    return [block, below, above, far_top, far_bottom]


def three_terms(value):
    first = lax.reduce_precision(value, 8, 7)
    rest = value - first
    second = lax.reduce_precision(rest, 8, 7)
    return first, second, rest - second


def corner(value, shape):
    row = lax.broadcasted_iota(jnp.int32, shape, 0)
    col = lax.broadcasted_iota(jnp.int32, shape, 1)
    out = jnp.zeros(shape, F32)
    for k, term in enumerate(three_terms(value)):
        out = jnp.where((row == k) & (col == 0), term, out)
    return out.astype(BF16)


def score_kernel(
    place, slot, ein, ql,
    own_0, own_1, own_2, own_top, own_bottom,
    near_0, near_1, near_2, near_top, near_bottom,
    last_0, last_1, last_2, last_top, last_bottom,
    eig, out, inverse, left, right, own_3, near_3, last_3, grads,
):
    n = pl.program_id(0)
    dj = eig.shape[1]
    size = own_0.shape[0]
    blocks = []
    for own, near, last in (
        (own_0, near_0, last_0),
        (own_1, near_1, last_1),
        (own_2, near_2, last_2),
        (own_3, near_3, last_3),
    ):
        blocks += [(own, 0), (near, 0), (near, size), (last, 0)]
    after = NSEQ * 32

    @pl.when(n == 0)
    def _():
        for far, top, bottom in (
            (own_3, own_top, own_bottom),
            (near_3, near_top, near_bottom),
            (last_3, last_top, last_bottom),
        ):
            far[: top.shape[0], :] = top[...]
            far[top.shape[0] :, :] = bottom[...]
        for k, (ref, row) in enumerate(blocks):
            start = pl.multiple_of(place[k] * 64, 64)
            right[pl.ds(start, 64), :] = ref[row + after : row + after + 64, :dj]
        total = jnp.sum(ql[:, :, 64:].astype(F32))
        inverse[...] = 1.0 / (eig[...] + (0.1 / (D * H)) * total)
        for e in range(NSEQ):
            left[64 * e : 64 * e + 64, :] = ql[e].T[:64, :]
        out[...] = jnp.zeros_like(out)

    first = pl.multiple_of(slot[n] * 32, 32)
    for k, (ref, row) in enumerate(blocks):
        start = pl.multiple_of(place[k] * 16, 16)
        rows = ref[pl.ds(row + first, 32), :]
        grads[pl.ds(start, 16), :] = rows[:16]
        grads[256 + 16 * k : 256 + 16 * k + 16, :] = rows[16:]
    pair = jnp.dot(ein[0], grads[...], preferred_element_type=F32)[:, :dj]
    scaled = (pair * inverse[...]).astype(BF16)
    width = scaled.shape[1]
    sums = []
    for k in range(4):
        part = jnp.dot(left[256 * k : 256 * k + 256, :], scaled, preferred_element_type=F32)
        part = part * right[256 * k : 256 * k + 256, :].astype(F32)
        sums.append(jnp.sum(part.reshape(8, RANK, width), axis=1))
    total = jnp.sum(jnp.concatenate(sums, 0), axis=1, keepdims=True)
    lane = lax.broadcasted_iota(jnp.int32, out.shape, 1)
    out[...] = jnp.where(lane == n, total, out[...])


def score_call(place, slot, ein, blocks, eigvals):
    di, dj = eigvals.shape

    def whole(x):
        return pl.BlockSpec(x.shape, lambda n, rank=x.ndim: (0,) * rank)

    return pl.pallas_call(
        score_kernel,
        grid=(NSEQ,),
        in_specs=[pl.BlockSpec(memory_space=pltpu.SMEM)] * 2
        + [
            pl.BlockSpec((1, di, SEQLEN), lambda n: (n, 0, 0)),
            pl.BlockSpec((16, di, 128), lambda n: (0, 0, 4)),
        ]
        + [whole(x) for x in (*blocks, eigvals)],
        out_specs=pl.BlockSpec((QUERIES, 128), lambda n: (0, 0)),
        out_shape=jax.ShapeDtypeStruct((QUERIES, 128), F32),
        scratch_shapes=[
            pltpu.VMEM((di, dj), F32),
            pltpu.VMEM((16 * 64, di), BF16),
            pltpu.VMEM((16 * 64, dj), BF16),
            pltpu.VMEM(blocks[0].shape, BF16),
            pltpu.VMEM(blocks[5].shape, BF16),
            pltpu.VMEM(blocks[10].shape, BF16),
            pltpu.VMEM((SEQLEN, blocks[0].shape[1]), BF16),
        ],
        compiler_params=pltpu.CompilerParams(vmem_limit_bytes=48 * 1024 * 1024),
        cost_estimate=pl.CostEstimate(
            flops=10_000_000_000, bytes_accessed=16_000_000, transcendentals=0
        ),
    )(place, slot, ein, ein, *blocks, eigvals)


def shards(train_in, train_grad, seq_lens, basis_in, basis_out, eigvals, query_in, query_out):
    me = lax.axis_index("shard")
    example = lax.axis_index("example")
    place = jnp.stack(
        [(me // 4 + dz) % 4 * 4 + (me % 4 + dy) % 4 for dy in AWAY for dz in AWAY]
    ).astype(jnp.int32)
    seq = jnp.arange(NSEQ, dtype=jnp.int32)
    x_off = (seq // 2 - example // 2) % 4
    x_slot = jnp.where(x_off == 0, 0, jnp.where(x_off == 3, 1, jnp.where(x_off == 1, 2, 3)))
    slot = (
        ((seq % 2) != (example % 2)).astype(jnp.int32) * 8
        + x_slot * 2
        + ((seq // 8) != (example // 8)).astype(jnp.int32)
    ).astype(jnp.int32)
    di, dj = eigvals.shape
    row_major = Layout(major_to_minor=(0, 1))

    rows_all = lax.all_gather(
        jnp.concatenate([train_in[0, :16], corner(jnp.sum(eigvals), (16, 128))], 1),
        "shard",
        axis=0,
    )
    rows_ring = jnp.concatenate(ring4(train_in[0, 16:], "shard", SHARD_Z, 8), 0)
    rows_y = ring4(rows_ring, "shard", SHARD_Y, 32)
    rows_ring = jnp.concatenate(rows_y, 0)

    block = jnp.concatenate([train_grad[0], lax.ppermute(train_grad[0], "example", EXAMPLE_Z)], 0)
    block = jnp.concatenate(ring4(block, "example", EXAMPLE_X, 32), 0)
    other = lax.ppermute(block, "example", EXAMPLE_CORE)
    query_right = jnp.dot(
        jnp.where(jnp.isnan(rows_y[1][0, 0]), jnp.zeros((64, H), BF16), query_out.reshape(64, H)),
        basis_out,
        preferred_element_type=F32,
    ).astype(BF16)
    part_out = [
        jnp.dot(b, basis_out, preferred_element_type=F32).astype(BF16)
        for b in (block, other)
    ]
    part_out = jnp.concatenate(part_out + [query_right], 0)
    part_out = with_layout_constraint(jnp.pad(part_out, ((0, 0), (0, 512 - dj))), row_major)
    z_blocks = ring4(part_out, "shard", SHARD_Z, 288)
    near = jnp.concatenate(z_blocks[1:3], 0)
    last = jnp.concatenate(z_blocks[3:], 0)
    blocks = (
        ring4(part_out, "shard", SHARD_Y, 288)
        + ring4(near, "shard", SHARD_Y, 576)
        + ring4(last, "shard", SHARD_Y, 288)
    )

    own_in = jnp.concatenate(
        [
            jnp.dot(rows, basis_in, preferred_element_type=F32)
            for rows in (rows_all[:, :, :D].reshape(256, D), rows_ring)
        ],
        0,
    )
    half = jnp.arange(16, dtype=jnp.int32)
    token = jnp.concatenate(
        [(half[:, None] * 32 + half).reshape(256), (place[:, None] * 32 + 16 + half).reshape(256)]
    )
    own_in = jnp.where(token[:, None] < seq_lens[0], own_in, 0.0).astype(BF16)
    query_left = jnp.dot(
        jnp.where(jnp.isnan(rows_y[1][0, 0]), jnp.zeros((64, D), BF16), query_in.reshape(64, D)),
        basis_in,
        preferred_element_type=F32,
    ).astype(BF16)
    eig_shard = corner(jnp.sum(rows_all[:, :, D:].astype(F32)), (di, 64))
    ein = jnp.concatenate([own_in.T, query_left.T, eig_shard], 1)
    flag = jnp.isnan(sum(b[0, 0] for b in z_blocks[1:3] + blocks[1:3]))
    ein = jnp.where(flag, jnp.zeros_like(ein), ein)
    ein = lax.all_gather(ein, "example", axis=0)

    partial = score_call(place, slot, ein, blocks, eigvals)[:, :NSEQ]
    pieces = partial.reshape(16, 2, 16).transpose(0, 2, 1).reshape(256, 2)
    pieces = lax.all_to_all(pieces, ("shard", "example"), 0, 0, tiled=True)
    normalizer = 1.0 / math.sqrt(RANK * D * H * SEQLEN)
    return (jnp.sum(pieces, axis=0) * normalizer).reshape(2, 1)


def solution(mesh):
    placed = (
        P("example", "shard", None),
        P("example", "shard", None),
        P("example"),
        P(None, "shard"),
        P(None, "example"),
        P("shard", "example"),
        P("example", None, None),
        P("shard", None, None),
    )
    return jax.shard_map(
        shards, mesh=mesh, in_specs=placed, out_specs=P("shard", "example"), check_vma=False
    )
```
